32 devices in a mesh: clips: 2 (over y), patch: 16 (over z, x, core).
Axes of the slice: x: 2, y: 2, z: 4, core: 2. Of those that a mesh axis runs over, the one named last changes fastest.
Arguments:
- queries: bfloat16 [1024, 2560], P(('clips', 'patch')), parts along dimension 0, may hold values from -130 to 130
- keys_new: bfloat16 [1024, 2560], P(('clips', 'patch')), parts along dimension 0, may hold values from -6 to 6
- values_new: bfloat16 [1024, 2560], P(('clips', 'patch')), parts along dimension 0, may hold values from -6 to 6
- keys_copy: bfloat16 [32, 512, 640], P(('clips', 'patch')), parts along dimension 0, may hold values from -6 to 6, as said below
- values_copy: bfloat16 [32, 512, 640], P(('clips', 'patch')), parts along dimension 0, may hold values from -6 to 6, as said below
- key_bounds: float32 [1024, 20], P('clips'), parts along dimension 0, may hold values from 0.5 to 3
- value_bounds: float32 [1024, 20], P('clips'), parts along dimension 0, may hold values from 0.5 to 3
Outputs:
- attended: bfloat16 [1024, 2560], P(('clips', 'patch')), parts along dimension 0
The draws below stay inside these ranges and needn't reach their ends.
There are 2 independent parts, one for each index of `clips`. The reference program is written for one: setup_inputs(seed, part) draws one part's arguments, and reference() takes and returns one part's arrays. A program takes and returns all parts, laid end to end along the dimension named above; each array names one. Nothing has to cross between parts.
Inputs may be any that keep to these rules, and one draw needn't show every extreme that they name: `keys_copy`: copies p and q are equal when p % 4 == q % 4; copy p holds features (p % 4) * 640 onward of one previous-step key array. `values_copy`: copies p and q are equal when p % 4 == q % 4; copy p holds features (p % 4) * 640 onward of one previous-step value array.
All inputs are finite; a program needn't handle non-finite values.
Results may differ from the reference program's by a relative error of at most 0.0083.
Values may be sent and summed in bfloat16 or wider, within the bound.
No kernel may reach another device: no remote copies, remote signals or barrier semaphores. Data moves between devices by JAX's collectives and lax.ppermute only.
A program may use at most 128 MiB of HBM per device.

```python
import math
import jax
import jax.numpy as jnp
from jax import lax

HEADS = 20
HD = 128
TOK_DEV = 32
TOKENS = 512
F = 2560
N_PATCH = 16


def shared_keys(key):
    return jnp.clip(jax.random.normal(key, (TOKENS, HEADS * HD), jnp.float32), -6.0, 6.0)


def copies_from(key):
    common = jnp.clip(jax.random.normal(key, (TOKENS, HEADS * HD), jnp.float32), -6.0, 6.0)
    quarters = common.reshape(TOKENS, 4, HEADS * HD // 4).transpose(1, 0, 2)
    return jnp.tile(quarters, (N_PATCH // 4, 1, 1))


def draw_keys_new(key, part):
    return shared_keys(key).astype(jnp.bfloat16)


def draw_keys_copy(key, part):
    key = jax.random.fold_in(key, 3)
    return copies_from(key).astype(jnp.bfloat16)


def draw_values_copy(key, part):
    key = jax.random.fold_in(key, 5)
    return copies_from(key).astype(jnp.bfloat16)


def draw_queries(key, part):
    key = jax.random.fold_in(key, 7)
    fresh = jnp.clip(1.5 * jax.random.normal(key, (TOKENS, HEADS * HD), jnp.float32), -9.0, 9.0)
    return fresh.astype(jnp.bfloat16)


def levels(key, dims, pieces, least, top_value):
    def one(axis_at, blocks):
        draws = jax.random.uniform(jax.random.fold_in(jax.random.fold_in(key, 6), axis_at), (blocks,), jnp.float32, least / len(pieces), top_value / len(pieces))
        return jnp.repeat(jnp.exp(draws), dims[axis_at] // blocks).reshape((-1,) + (1,) * (len(dims) - axis_at - 1))

    loudness = one(*pieces[0])
    for cut in pieces[1:]:
        loudness = loudness * one(*cut)
    return loudness


def bell_draw(own_key, shape, scale, most, pieces=(), kind=jnp.bfloat16):
    result = scale * jax.random.normal(own_key, shape, jnp.float32)
    if pieces:
        result = result * levels(own_key, shape, pieces, -0.22, 0.18)
    return jnp.clip(result, -most, most).astype(kind)


def setup_inputs(seed: int = 0, part: int = 0) -> dict:
    keys = jax.random.split(jax.random.key(seed), 8)
    own_keys = jax.random.split(jax.random.fold_in(keys[7], part), 8)
    return {
        "queries": draw_queries(jax.random.fold_in(jax.random.fold_in(keys[7], part), 71), part),
        "keys_new": draw_keys_new(jax.random.fold_in(jax.random.fold_in(keys[7], part), 71), part),
        "values_new": bell_draw(own_keys[2], (TOKENS, F), 1.0, 6.0, ((0, 16),)),
        "keys_copy": draw_keys_copy(jax.random.fold_in(jax.random.fold_in(keys[7], part), 71), part),
        "values_copy": draw_values_copy(jax.random.fold_in(jax.random.fold_in(keys[7], part), 71), part),
        "key_bounds": jnp.clip(jnp.exp(jax.random.uniform(own_keys[5], (TOKENS, HEADS), jnp.float32, math.log(0.5), math.log(3.0))), 0.5, 3.0),
        "value_bounds": jnp.clip(jnp.exp(jax.random.uniform(own_keys[6], (TOKENS, HEADS), jnp.float32, math.log(0.5), math.log(3.0))), 0.5, 3.0),
    }


def rebuild(current, previous, bounds):
    limits = jnp.repeat(bounds, HD, axis=1)
    change = jnp.clip(current.astype(jnp.float32) - previous.astype(jnp.float32), -limits, limits).astype(jnp.bfloat16)
    return (previous.astype(jnp.float32) + change.astype(jnp.float32)).astype(jnp.bfloat16)


def one_head(operands):
    query_h, key_h, value_h = operands
    scores = jnp.dot(query_h, key_h.T, preferred_element_type=jnp.float32) * (HD ** -0.5)
    peaks = jnp.max(scores, axis=1, keepdims=True)
    probs = jnp.exp(scores - peaks)
    totals = jnp.sum(probs, axis=1, keepdims=True)
    weighted = jnp.dot(probs.astype(jnp.bfloat16), value_h, preferred_element_type=jnp.float32)
    return (weighted / totals).astype(jnp.bfloat16)


def reference(queries, keys_new, values_new, keys_copy, values_copy, key_bounds, value_bounds):
    group_rows = 4 * TOK_DEV
    quarter_width = HEADS * HD // 4
    quarter_heads = HEADS // 4

    def one_device(place):
        member = place % 4
        group = place // 4
        column = (member * quarter_width).astype(jnp.int32)
        head_start = (member * quarter_heads).astype(jnp.int32)
        row_start = (group * group_rows).astype(jnp.int32)
        query_part = lax.dynamic_slice(queries, (row_start, column), (group_rows, quarter_width))
        key_part = lax.dynamic_slice_in_dim(keys_new, column, quarter_width, 1)
        value_part = lax.dynamic_slice_in_dim(values_new, column, quarter_width, 1)
        key_limits = lax.dynamic_slice_in_dim(key_bounds, head_start, quarter_heads, 1)
        value_limits = lax.dynamic_slice_in_dim(value_bounds, head_start, quarter_heads, 1)
        keys_used = rebuild(key_part, lax.dynamic_index_in_dim(keys_copy, place, 0, keepdims=False), key_limits)
        values_used = rebuild(value_part, lax.dynamic_index_in_dim(values_copy, place, 0, keepdims=False), value_limits)
        query_heads = query_part.reshape(group_rows, quarter_heads, HD).transpose(1, 0, 2)
        key_heads = keys_used.reshape(TOKENS, quarter_heads, HD).transpose(1, 0, 2)
        value_heads = values_used.reshape(TOKENS, quarter_heads, HD).transpose(1, 0, 2)
        outputs = lax.map(one_head, (query_heads, key_heads, value_heads))
        return outputs.transpose(1, 0, 2).reshape(group_rows, quarter_width)

    blocks = lax.map(one_device, jnp.arange(N_PATCH, dtype=jnp.int32))
    blocks = blocks.reshape(N_PATCH // 4, 4, group_rows, quarter_width).transpose(0, 2, 1, 3)
    return blocks.reshape(TOKENS, HEADS * HD)
```

```python
import functools

import jax
import jax.numpy as jnp
from jax import lax
from jax.experimental import pallas as pl
from jax.experimental.pallas import tpu as pltpu
from jax.sharding import PartitionSpec as P

GROUP = 4
STAT_ROWS = 16
LOG2E = 1.4426950408889634
HBM = pl.BlockSpec(memory_space=pl.ANY)
VMEM = pl.BlockSpec(memory_space=pltpu.VMEM)


def swapped(array, mask):
    size = lax.axis_size("patch")
    return lax.ppermute(array, "patch", [(i, i ^ mask) for i in range(size)])


def position():
    place = lax.axis_index("patch")
    return place // GROUP, place % GROUP


def columns(member, width):
    return pl.ds(pl.multiple_of(member * width, width), width)


def run_copies(pairs, sems):
    copies = [pltpu.make_async_copy(a, b, sems.at[i]) for i, (a, b) in enumerate(pairs)]
    for copy in copies:
        copy.start()
    for copy in copies:
        copy.wait()


def cut_kernel(count, *refs):
    slabs, outs, sems = refs[:count], refs[count:-1], refs[-1]
    width = slabs[0].shape[1] // GROUP
    _, member = position()
    pairs = []
    for k in range(1, GROUP):
        for i, slab in enumerate(slabs):
            pairs.append((slab.at[:, columns(member ^ k, width)], outs[k - 1].at[i]))
    run_copies(pairs, sems)


def cut(*slabs):
    rows, features = slabs[0].shape
    shape = jax.ShapeDtypeStruct((len(slabs), rows, features // GROUP), slabs[0].dtype)
    return pl.pallas_call(
        functools.partial(cut_kernel, len(slabs)),
        out_shape=[shape] * (GROUP - 1),
        in_specs=[HBM] * len(slabs),
        out_specs=[HBM] * (GROUP - 1),
        scratch_shapes=[pltpu.SemaphoreType.DMA((len(slabs) * (GROUP - 1),))],
        cost_estimate=pl.CostEstimate(flops=0, bytes_accessed=1_500_000, transcendentals=0),
        name="cut",
    )(*slabs)


def rebuild_kernel(
    heads, keys_ref, values_ref, a1, a2, a3, keys_copy, values_copy, kb, vb, out, own, old, sems
):
    rows, features = keys_ref.shape
    width = features // GROUP
    head = width // heads
    group, member = position()
    pairs = []
    for i, (slab, copy) in enumerate(((keys_ref, keys_copy), (values_ref, values_copy))):
        pairs.append((slab.at[:, columns(member, width)], own.at[i]))
        start = pl.multiple_of(group * GROUP * rows, GROUP * rows)
        pairs.append((copy.at[0, pl.ds(start, GROUP * rows), :], old.at[i]))
    run_copies(pairs, sems)
    for k, piece in enumerate((own, a1, a2, a3)):
        place = pl.ds(pl.multiple_of((member ^ k) * rows, rows), rows)
        for i, bounds in enumerate((kb, vb)):
            limits = bounds[place, :]
            for h in range(heads):
                lanes = slice(h * head, (h + 1) * head)
                limit = limits[:, h : h + 1]
                previous = old[i, place, lanes].astype(jnp.float32)
                change = jnp.clip(piece[i, :, lanes].astype(jnp.float32) - previous, -limit, limit)
                change = change.astype(jnp.bfloat16).astype(jnp.float32)
                out[i, k * rows : (k + 1) * rows, lanes] = (previous + change).astype(out.dtype)


def rebuild(heads, keys_new, values_new, arrived, keys_copy, values_copy, kb, vb):
    rows, features = keys_new.shape
    width = features // GROUP
    return pl.pallas_call(
        functools.partial(rebuild_kernel, heads),
        out_shape=jax.ShapeDtypeStruct((2, GROUP * rows, width), keys_new.dtype),
        in_specs=[HBM] * 2 + [VMEM] * 3 + [HBM] * 2 + [VMEM] * 2,
        out_specs=VMEM,
        scratch_shapes=[
            pltpu.VMEM((2, rows, width), keys_new.dtype),
            pltpu.VMEM((2, GROUP * rows, width), keys_new.dtype),
            pltpu.SemaphoreType.DMA((4,)),
        ],
        cost_estimate=pl.CostEstimate(flops=0, bytes_accessed=3_000_000, transcendentals=0),
        name="rebuild",
    )(keys_new, values_new, *arrived, keys_copy, values_copy, kb, vb)


def attend_kernel(heads, slab, q1, q2, q3, near, far, o0, o1, o2, o3, own, sem):
    rows, features = slab.shape
    width = features // GROUP
    head = width // heads
    _, member = position()
    run_copies([(slab.at[:, columns(member, width)], own)], sem)
    scale = head ** (-0.5) * LOG2E
    lane = lax.broadcasted_iota(jnp.int32, (GROUP * rows, head), 1)
    stats = jnp.zeros((GROUP * rows, head), jnp.float32)
    contract = (((1,), (1,)), ((), ()))
    outs = (o0, o1, o2, o3)
    for h in range(heads):
        lanes = slice(h * head, (h + 1) * head)
        query = jnp.concatenate([own[:, lanes], q1[0, :, lanes], q2[0, :, lanes], q3[0, :, lanes]], axis=0)
        scores = [
            lax.dot_general(query, block[0, :, lanes], contract, preferred_element_type=jnp.float32)
            for block in (near, far)
        ]
        peak = jnp.maximum(
            jnp.max(scores[0], axis=1, keepdims=True), jnp.max(scores[1], axis=1, keepdims=True)
        )
        level = (peak * scale).astype(jnp.bfloat16).astype(jnp.float32)
        total = None
        for block, score in zip((near, far), scores):
            probs = jnp.exp2(score * scale - level).astype(jnp.bfloat16)
            value = block[1, :, lanes]
            joined = jnp.concatenate([value, jnp.ones_like(value)], axis=1)
            part = jnp.dot(probs, joined, preferred_element_type=jnp.float32)
            total = part if total is None else total + part
        weighted = total[:, :head].astype(jnp.bfloat16)
        weight = total[:, head:]
        high = weight.astype(jnp.bfloat16).astype(jnp.float32)
        stats = jnp.where(lane == h, level, stats)
        stats = jnp.where(lane == heads + h, high, stats)
        stats = jnp.where(lane == 2 * heads + h, weight - high, stats)
        for k, out in enumerate(outs):
            out[h * rows : (h + 1) * rows, :] = weighted[k * rows : (k + 1) * rows]
    half = rows // 2
    for k, out in enumerate(outs):
        first = stats[k * rows : k * rows + half]
        second = stats[k * rows + half : (k + 1) * rows]
        packed = first + pltpu.roll(second, 16, 1)
        out[heads * rows :, :] = packed.astype(out.dtype)


def attend(heads, slab, pieces, near, far):
    rows, features = slab.shape
    width = features // GROUP
    head = width // heads
    out = jax.ShapeDtypeStruct((heads * rows + rows // 2, head), slab.dtype)
    return pl.pallas_call(
        functools.partial(attend_kernel, heads),
        out_shape=[out] * GROUP,
        in_specs=[HBM] + [VMEM] * 5,
        out_specs=[VMEM] * GROUP,
        scratch_shapes=[
            pltpu.VMEM((rows, width), slab.dtype),
            pltpu.SemaphoreType.DMA((1,)),
        ],
        compiler_params=pltpu.CompilerParams(vmem_limit_bytes=48 * 1024 * 1024),
        cost_estimate=pl.CostEstimate(flops=0, bytes_accessed=5_000_000, transcendentals=0),
        name="attend",
    )(slab, *pieces, near, far)


def merge_kernel(heads, n0, n1, n2, n3, f0, f1, f2, f3, out):
    rows = out.shape[0]
    head = n0.shape[1]
    width = heads * head
    half = rows // 2
    _, member = position()

    def unpack(ref):
        packed = ref[heads * rows :, :].astype(jnp.float32)
        stats = jnp.concatenate([packed, pltpu.roll(packed, head - 16, 1)], axis=0)
        weight = pltpu.roll(stats, head - heads, 1) + pltpu.roll(stats, head - 2 * heads, 1)
        return stats, weight

    for k, (near, far) in enumerate(((n0, f0), (n1, f1), (n2, f2), (n3, f3))):
        near_level, near_weight = unpack(near)
        far_level, far_weight = unpack(far)
        top = jnp.maximum(near_level, far_level)
        near_scale = jnp.exp2(near_level - top)
        far_scale = jnp.exp2(far_level - top)
        total = near_scale * near_weight + far_scale * far_weight
        near_scale = near_scale / total
        far_scale = far_scale / total
        for h in range(heads):
            part = slice(h * rows, (h + 1) * rows)
            mixed = near[part, :].astype(jnp.float32) * near_scale[:, h : h + 1]
            mixed = mixed + far[part, :].astype(jnp.float32) * far_scale[:, h : h + 1]
            start = pl.multiple_of((member ^ k) * width + h * head, head)
            out[:, pl.ds(start, head)] = mixed.astype(out.dtype)


def merge(heads, near, far, rows):
    head = near[0].shape[1]
    return pl.pallas_call(
        functools.partial(merge_kernel, heads),
        out_shape=jax.ShapeDtypeStruct((rows, GROUP * heads * head), near[0].dtype),
        in_specs=[VMEM] * 8,
        out_specs=VMEM,
        cost_estimate=pl.CostEstimate(flops=0, bytes_accessed=2_000_000, transcendentals=0),
        name="merge",
    )(*near, *far)


def shards(queries, keys_new, values_new, keys_copy, values_copy, key_bounds, value_bounds):
    rows = queries.shape[0]
    heads = key_bounds.shape[1] // GROUP
    levels = lax.axis_size("patch").bit_length() - 1
    across = 1 << levels - 1
    group, member = position()

    far_slab = swapped(queries, across)
    kv_sent = cut(keys_new, values_new)
    arrived = [swapped(kv_sent[k - 1], k) for k in range(1, GROUP)]
    corner = (group * GROUP * rows, member * heads)
    limits = [lax.dynamic_slice(b, corner, (GROUP * rows, heads)) for b in (key_bounds, value_bounds)]
    near = rebuild(heads, keys_new, values_new, arrived, keys_copy, values_copy, *limits)
    for bit in range(2, levels - 2):
        near = jnp.concatenate([near, swapped(near, 1 << bit)], axis=1)
    far = swapped(near, 1 << levels - 2)
    own_sent = cut(queries)
    own_pieces = [swapped(own_sent[k - 1], k) for k in range(1, GROUP)]
    far_sent = cut(far_slab)
    far_pieces = [swapped(far_sent[k - 1], k) for k in range(1, GROUP)]
    far_out = attend(heads, far_slab, far_pieces, near, far)
    far_back = [swapped(far_out[k], across + k) for k in range(GROUP)]
    own_out = attend(heads, queries, own_pieces, near, far)
    own_back = [own_out[0]] + [swapped(own_out[k], k) for k in range(1, GROUP)]
    return merge(heads, own_back, far_back, rows)


def solution(mesh):
    rows = P(("clips", "patch"), None)
    copies = P(("clips", "patch"), None, None)
    bounds = P("clips", None)
    return jax.shard_map(
        shards,
        mesh=mesh,
        in_specs=(rows, rows, rows, copies, copies, bounds, bounds),
        out_specs=rows,
        check_vma=False,
    )
```

```python
import functools

import jax
import jax.numpy as jnp
from jax import lax
from jax.experimental import pallas as pl
from jax.experimental.pallas import tpu as pltpu
from jax.sharding import PartitionSpec as P

GROUP = 4
STAT_ROWS = 16
LOG2E = 1.4426950408889634
HBM = pl.BlockSpec(memory_space=pl.ANY)
VMEM = pl.BlockSpec(memory_space=pltpu.VMEM)


MB = 1 << 20


def limit(size):
    return pltpu.CompilerParams(vmem_limit_bytes=size)


def cost(size):
    return pl.CostEstimate(flops=0, bytes_accessed=size, transcendentals=0)


def swapped(array, mask):
    size = lax.axis_size("patch")
    return lax.ppermute(array, "patch", [(i, i ^ mask) for i in range(size)])


def position():
    place = lax.axis_index("patch")
    return place // GROUP, place % GROUP


def columns(member, width):
    return pl.ds(pl.multiple_of(member * width, width), width)


def run_copies(pairs, sems):
    copies = [pltpu.make_async_copy(a, b, sems.at[i]) for i, (a, b) in enumerate(pairs)]
    for copy in copies:
        copy.start()
    for copy in copies:
        copy.wait()


def cut_kernel(count, *refs):
    slabs, outs = refs[:count], refs[count:]
    width = slabs[0].shape[1] // GROUP
    _, member = position()
    for k in range(1, GROUP):
        for i, slab in enumerate(slabs):
            outs[k - 1][i] = slab[:, columns(member ^ k, width)]


def cut(*slabs):
    rows, features = slabs[0].shape
    shape = jax.ShapeDtypeStruct((len(slabs), rows, features // GROUP), slabs[0].dtype)
    return pl.pallas_call(
        functools.partial(cut_kernel, len(slabs)),
        out_shape=[shape] * (GROUP - 1),
        in_specs=[VMEM] * len(slabs),
        out_specs=[VMEM] * (GROUP - 1),
        compiler_params=limit(4 * MB),
        cost_estimate=cost(1000),
        name="cut",
    )(*slabs)


def rebuild_kernel(
    heads, keys_ref, values_ref, a1, a2, a3, keys_copy, values_copy, kb, vb, out, own, old, bounds, sems
):
    rows, features = keys_ref.shape
    width = features // GROUP
    head = width // heads
    group, member = position()
    pairs = []
    start = pl.multiple_of(group * GROUP * rows, GROUP * rows)
    block = pl.ds(start, GROUP * rows)
    for i, (slab, copy, bound) in enumerate(((keys_ref, keys_copy, kb), (values_ref, values_copy, vb))):
        pairs.append((slab.at[:, columns(member, width)], own.at[i]))
        pairs.append((copy.at[0, block, :], old.at[i]))
        pairs.append((bound.at[block, :], bounds.at[i]))
    run_copies(pairs, sems)
    lane = lax.broadcasted_iota(jnp.int32, (rows, bounds.shape[2]), 1)
    for k, piece in enumerate((own, a1, a2, a3)):
        place = pl.ds(pl.multiple_of((member ^ k) * rows, rows), rows)
        for i in range(2):
            limits = bounds[i, place, :]
            for h in range(heads):
                lanes = slice(h * head, (h + 1) * head)
                chosen = jnp.where(lane == member * heads + h, limits, 0.0)
                limit = jnp.sum(chosen, axis=1, keepdims=True)
                previous = old[i, place, lanes].astype(jnp.float32)
                change = jnp.clip(piece[i, :, lanes].astype(jnp.float32) - previous, -limit, limit)
                change = change.astype(jnp.bfloat16).astype(jnp.float32)
                out[i, k * rows : (k + 1) * rows, lanes] = (previous + change).astype(out.dtype)


def rebuild(heads, keys_new, values_new, arrived, keys_copy, values_copy, kb, vb):
    rows, features = keys_new.shape
    width = features // GROUP
    return pl.pallas_call(
        functools.partial(rebuild_kernel, heads),
        out_shape=jax.ShapeDtypeStruct((2, GROUP * rows, width), keys_new.dtype),
        in_specs=[HBM] * 2 + [VMEM] * 3 + [HBM] * 4,
        out_specs=VMEM,
        scratch_shapes=[
            pltpu.VMEM((2, rows, width), keys_new.dtype),
            pltpu.VMEM((2, GROUP * rows, width), keys_new.dtype),
            pltpu.VMEM((2, GROUP * rows, kb.shape[1]), kb.dtype),
            pltpu.SemaphoreType.DMA((6,)),
        ],
        compiler_params=limit(8 * MB),
        cost_estimate=cost(1000),
        name="rebuild",
    )(keys_new, values_new, *arrived, keys_copy, values_copy, kb, vb)


def attend_kernel(heads, slab, q1, q2, q3, near, far, o0, o1, o2, o3, own, sem):
    rows, features = slab.shape
    width = features // GROUP
    head = width // heads
    _, member = position()
    run_copies([(slab.at[:, columns(member, width)], own)], sem)
    scale = head ** (-0.5) * LOG2E
    lane = lax.broadcasted_iota(jnp.int32, (GROUP * rows, head), 1)
    stats = jnp.zeros((GROUP * rows, head), jnp.float32)
    contract = (((1,), (1,)), ((), ()))
    outs = (o0, o1, o2, o3)
    for h in range(heads):
        lanes = slice(h * head, (h + 1) * head)
        query = jnp.concatenate([own[:, lanes], q1[0, :, lanes], q2[0, :, lanes], q3[0, :, lanes]], axis=0)
        scores = [
            lax.dot_general(query, block[0, :, lanes], contract, preferred_element_type=jnp.float32)
            for block in (near, far)
        ]
        peak = jnp.maximum(
            jnp.max(scores[0], axis=1, keepdims=True), jnp.max(scores[1], axis=1, keepdims=True)
        )
        level = (peak * scale).astype(jnp.bfloat16).astype(jnp.float32)
        total = None
        for block, score in zip((near, far), scores):
            probs = jnp.exp2(score * scale - level).astype(jnp.bfloat16)
            value = block[1, :, lanes]
            joined = jnp.concatenate([value, jnp.ones_like(value)], axis=1)
            part = jnp.dot(probs, joined, preferred_element_type=jnp.float32)
            total = part if total is None else total + part
        weighted = total[:, :head].astype(jnp.bfloat16)
        weight = total[:, head:]
        high = weight.astype(jnp.bfloat16).astype(jnp.float32)
        stats = jnp.where(lane == h, level, stats)
        stats = jnp.where(lane == heads + h, high, stats)
        stats = jnp.where(lane == 2 * heads + h, weight - high, stats)
        for k, out in enumerate(outs):
            out[h * rows : (h + 1) * rows, :] = weighted[k * rows : (k + 1) * rows]
    half = rows // 2
    for k, out in enumerate(outs):
        first = stats[k * rows : k * rows + half]
        second = stats[k * rows + half : (k + 1) * rows]
        packed = first + pltpu.roll(second, 16, 1)
        out[heads * rows :, :] = packed.astype(out.dtype)


def attend(heads, slab, pieces, near, far):
    rows, features = slab.shape
    width = features // GROUP
    head = width // heads
    out = jax.ShapeDtypeStruct((heads * rows + rows // 2, head), slab.dtype)
    return pl.pallas_call(
        functools.partial(attend_kernel, heads),
        out_shape=[out] * GROUP,
        in_specs=[HBM] + [VMEM] * 5,
        out_specs=[VMEM] * GROUP,
        scratch_shapes=[
            pltpu.VMEM((rows, width), slab.dtype),
            pltpu.SemaphoreType.DMA((1,)),
        ],
        compiler_params=limit(4 * MB + 4 * near.size * near.dtype.itemsize + 32 * GROUP * rows * near.shape[1]),
        cost_estimate=cost(1000),
        name="attend",
    )(slab, *pieces, near, far)


def merge_kernel(heads, n0, n1, n2, n3, f0, f1, f2, f3, out):
    rows = out.shape[0]
    head = n0.shape[1]
    width = heads * head
    half = rows // 2
    _, member = position()

    def unpack(ref):
        packed = ref[heads * rows :, :].astype(jnp.float32)
        stats = jnp.concatenate([packed, pltpu.roll(packed, head - 16, 1)], axis=0)
        weight = pltpu.roll(stats, head - heads, 1) + pltpu.roll(stats, head - 2 * heads, 1)
        return stats, weight

    for k, (near, far) in enumerate(((n0, f0), (n1, f1), (n2, f2), (n3, f3))):
        near_level, near_weight = unpack(near)
        far_level, far_weight = unpack(far)
        top = jnp.maximum(near_level, far_level)
        near_scale = jnp.exp2(near_level - top)
        far_scale = jnp.exp2(far_level - top)
        total = near_scale * near_weight + far_scale * far_weight
        near_scale = near_scale / total
        far_scale = far_scale / total
        for h in range(heads):
            part = slice(h * rows, (h + 1) * rows)
            mixed = near[part, :].astype(jnp.float32) * near_scale[:, h : h + 1]
            mixed = mixed + far[part, :].astype(jnp.float32) * far_scale[:, h : h + 1]
            start = pl.multiple_of((member ^ k) * width + h * head, head)
            out[:, pl.ds(start, head)] = mixed.astype(out.dtype)


def merge(heads, near, far, rows):
    head = near[0].shape[1]
    return pl.pallas_call(
        functools.partial(merge_kernel, heads),
        out_shape=jax.ShapeDtypeStruct((rows, GROUP * heads * head), near[0].dtype),
        in_specs=[VMEM] * 8,
        out_specs=VMEM,
        compiler_params=limit(4 * MB),
        cost_estimate=cost(1000),
        name="merge",
    )(*near, *far)


def shards(queries, keys_new, values_new, keys_copy, values_copy, key_bounds, value_bounds):
    rows = queries.shape[0]
    heads = key_bounds.shape[1] // GROUP
    levels = lax.axis_size("patch").bit_length() - 1
    across = 1 << levels - 1

    far_slab = swapped(queries, across)
    kv_sent = cut(keys_new, values_new)
    arrived = [swapped(kv_sent[k - 1], k) for k in range(1, GROUP)]
    near = rebuild(heads, keys_new, values_new, arrived, keys_copy, values_copy, key_bounds, value_bounds)
    for bit in range(2, levels - 2):
        near = jnp.concatenate([near, swapped(near, 1 << bit)], axis=1)
    far = swapped(near, 1 << levels - 2)
    own_sent = cut(queries)
    own_pieces = [swapped(own_sent[k - 1], k) for k in range(1, GROUP)]
    far_sent = cut(far_slab)
    far_pieces = [swapped(far_sent[k - 1], k) for k in range(1, GROUP)]
    far_out = attend(heads, far_slab, far_pieces, near, far)
    far_back = [swapped(far_out[k], across + k) for k in range(GROUP)]
    own_out = attend(heads, queries, own_pieces, near, far)
    own_back = [own_out[0]] + [swapped(own_out[k], k) for k in range(1, GROUP)]
    return merge(heads, own_back, far_back, rows)


def solution(mesh):
    rows = P(("clips", "patch"), None)
    copies = P(("clips", "patch"), None, None)
    bounds = P("clips", None)
    return jax.shard_map(
        shards,
        mesh=mesh,
        in_specs=(rows, rows, rows, copies, copies, bounds, bounds),
        out_specs=rows,
        check_vma=False,
    )
```

```python
import functools

import jax
import jax.numpy as jnp
from jax import lax
from jax.experimental import pallas as pl
from jax.experimental.pallas import tpu as pltpu
from jax.sharding import PartitionSpec as P

GROUP = 4
LOG2E = 1.4426950408889634
MB = 1 << 20
HBM = pl.BlockSpec(memory_space=pltpu.HBM)
VMEM = pl.BlockSpec(memory_space=pltpu.VMEM)


def limit(size):
    return pltpu.CompilerParams(vmem_limit_bytes=size)


def cost(size):
    return pl.CostEstimate(flops=0, bytes_accessed=size, transcendentals=0)


def swapped(array, mask):
    size = lax.axis_size("patch")
    return lax.ppermute(array, "patch", [(i, i ^ mask) for i in range(size)])


def position():
    place = lax.axis_index("patch")
    return place // GROUP, place % GROUP


def part(index, size):
    return pl.ds(pl.multiple_of(index * size, size), size)


def run_copies(pairs, sems):
    copies = [pltpu.make_async_copy(a, b, sems.at[i]) for i, (a, b) in enumerate(pairs)]
    for copy in copies:
        copy.start()
    for copy in copies:
        copy.wait()


def cut_first_kernel(keys_ref, values_ref, o1, o2, o3, sems):
    width = keys_ref.shape[1] // GROUP
    _, member = position()
    pairs = []
    for k, out in enumerate((o1, o2, o3), 1):
        for i, slab in enumerate((keys_ref, values_ref)):
            pairs.append((slab.at[:, part(member ^ k, width)], out.at[i]))
    run_copies(pairs, sems)


def cut_kernel(first_ref, second_ref, o1, o2, o3):
    width = first_ref.shape[1] // GROUP
    _, member = position()
    for k, out in enumerate((o1, o2, o3), 1):
        for i, slab in enumerate((first_ref, second_ref)):
            out[i] = slab[:, part(member ^ k, width)]


def cut(first, second, from_hbm):
    rows, features = first.shape
    shape = jax.ShapeDtypeStruct((2, rows, features // GROUP), first.dtype)
    return pl.pallas_call(
        cut_first_kernel if from_hbm else cut_kernel,
        out_shape=[shape] * (GROUP - 1),
        in_specs=[HBM if from_hbm else VMEM] * 2,
        out_specs=[VMEM] * (GROUP - 1),
        scratch_shapes=[pltpu.SemaphoreType.DMA((6,))] if from_hbm else [],
        compiler_params=limit(4 * MB),
        cost_estimate=cost(1000),
        name="cut",
    )(first, second)


def fetch_kernel(
    heads, keys_ref, values_ref, keys_copy, values_copy, kb, vb, own, old, limits, lines, turned, sems
):
    rows, features = keys_ref.shape
    width = features // GROUP
    group, member = position()
    block = part(group, GROUP * rows)
    pairs = []
    for i, (slab, copy, bound) in enumerate(((keys_ref, keys_copy, kb), (values_ref, values_copy, vb))):
        pairs.append((bound.at[:, block], lines.at[i]))
        pairs.append((slab.at[:, part(member, width)], own.at[i]))
        for k in range(GROUP):
            source = copy.at[0, part(group * GROUP + (member ^ k), rows), :]
            pairs.append((source, old.at[i, pl.ds(k * rows, rows), :]))
    run_copies(pairs, sems)
    for i in range(2):
        chosen = lines[i, pl.ds(member * heads, heads), :]
        padding = jnp.zeros((limits.shape[2] - heads, GROUP * rows), chosen.dtype)
        turned[...] = jnp.concatenate([chosen, padding], axis=0).T
        for k in range(GROUP):
            limits[i, pl.ds(k * rows, rows), :] = turned[part(member ^ k, rows), :]


def fetch(heads, keys_new, values_new, keys_copy, values_copy, key_bounds, value_bounds):
    rows, features = keys_new.shape
    width = features // GROUP
    kind = keys_new.dtype
    return pl.pallas_call(
        functools.partial(fetch_kernel, heads),
        out_shape=[
            jax.ShapeDtypeStruct((2, rows, width), kind),
            jax.ShapeDtypeStruct((2, GROUP * rows, width), kind),
            jax.ShapeDtypeStruct((2, GROUP * rows, 128), key_bounds.dtype),
        ],
        in_specs=[HBM] * 6,
        out_specs=[VMEM] * 3,
        scratch_shapes=[
            pltpu.VMEM((2, key_bounds.shape[1], GROUP * rows), key_bounds.dtype),
            pltpu.VMEM((GROUP * rows, 128), key_bounds.dtype),
            pltpu.SemaphoreType.DMA((12,)),
        ],
        compiler_params=limit(4 * MB),
        cost_estimate=cost(1000),
        name="fetch",
    )(keys_new, values_new, keys_copy, values_copy, key_bounds.T, value_bounds.T)


def rebuild_kernel(heads, own, a1, a2, a3, old, limits, *outs):
    rows = own.shape[1]
    head = own.shape[2] // heads
    for k, piece in enumerate((own, a1, a2, a3)):
        place = slice(k * rows, (k + 1) * rows)
        for i in range(2):
            for h in range(heads):
                lanes = slice(h * head, (h + 1) * head)
                bound = limits[i, place, h : h + 1]
                previous = old[i, place, lanes].astype(jnp.float32)
                change = jnp.clip(piece[i, :, lanes].astype(jnp.float32) - previous, -bound, bound)
                change = change.astype(jnp.bfloat16).astype(jnp.float32)
                outs[i][place, lanes] = (previous + change).astype(outs[i].dtype)


def rebuild(heads, own, arrived, old, limits):
    return pl.pallas_call(
        functools.partial(rebuild_kernel, heads),
        out_shape=[jax.ShapeDtypeStruct(old.shape[1:], old.dtype)] * 2,
        in_specs=[VMEM] * 6,
        out_specs=[VMEM] * 2,
        compiler_params=limit(4 * MB),
        cost_estimate=cost(1000),
        name="rebuild",
    )(own, *arrived, old, limits)


def attend_kernel(heads, which, slab, q1, q2, q3, near_keys, near_values, far_keys, far_values, o0, o1, o2, o3):
    rows, features = slab.shape
    width = features // GROUP
    head = width // heads
    _, member = position()
    scale = head ** (-0.5) * LOG2E
    lane = lax.broadcasted_iota(jnp.int32, (GROUP * rows, head), 1)
    stats = jnp.zeros((GROUP * rows, head), jnp.float32)
    contract = (((1,), (1,)), ((), ()))
    outs = (o0, o1, o2, o3)
    for h in range(heads):
        lanes = slice(h * head, (h + 1) * head)
        own = slab[:, pl.ds(pl.multiple_of(member * width + h * head, head), head)]
        query = jnp.concatenate([own] + [q[which, :, lanes] for q in (q1, q2, q3)], axis=0)
        scores = [
            lax.dot_general(query, keys[:, lanes], contract, preferred_element_type=jnp.float32)
            for keys in (near_keys, far_keys)
        ]
        peak = jnp.maximum(
            jnp.max(scores[0], axis=1, keepdims=True), jnp.max(scores[1], axis=1, keepdims=True)
        )
        level = (peak * scale).astype(jnp.bfloat16).astype(jnp.float32)
        total = None
        for values, score in zip((near_values, far_values), scores):
            probs = jnp.exp2(score * scale - level).astype(jnp.bfloat16)
            value = values[:, lanes]
            joined = jnp.concatenate([value, jnp.ones_like(value)], axis=1)
            product = jnp.dot(probs, joined, preferred_element_type=jnp.float32)
            total = product if total is None else total + product
        weighted = total[:, :head].astype(jnp.bfloat16)
        weight = total[:, head:]
        high = weight.astype(jnp.bfloat16).astype(jnp.float32)
        stats = jnp.where(lane == h, level, stats)
        stats = jnp.where(lane == heads + h, high, stats)
        stats = jnp.where(lane == 2 * heads + h, weight - high, stats)
        for k, out in enumerate(outs):
            out[h * rows : (h + 1) * rows, :] = weighted[k * rows : (k + 1) * rows]
    half = rows // 2
    for k, out in enumerate(outs):
        first = stats[k * rows : k * rows + half]
        second = stats[k * rows + half : (k + 1) * rows]
        packed = first + pltpu.roll(second, 16, 1)
        out[heads * rows :, :] = packed.astype(out.dtype)


def attend(heads, which, slab, pieces, near, far):
    rows, features = slab.shape
    width = features // GROUP
    head = width // heads
    out = jax.ShapeDtypeStruct((heads * rows + rows // 2, head), slab.dtype)
    room = 4 * MB + 8 * near[0].size * near[0].dtype.itemsize + 32 * GROUP * rows * near[0].shape[0]
    return pl.pallas_call(
        functools.partial(attend_kernel, heads, which),
        out_shape=[out] * GROUP,
        in_specs=[VMEM] * 8,
        out_specs=[VMEM] * GROUP,
        compiler_params=limit(room),
        cost_estimate=cost(1000),
        name="attend",
    )(slab, *pieces, *near, *far)


def merge_kernel(heads, n0, n1, n2, n3, f0, f1, f2, f3, out):
    rows = out.shape[0]
    head = n0.shape[1]
    width = heads * head
    _, member = position()

    def unpack(ref):
        packed = ref[heads * rows :, :].astype(jnp.float32)
        stats = jnp.concatenate([packed, pltpu.roll(packed, head - 16, 1)], axis=0)
        weight = pltpu.roll(stats, head - heads, 1) + pltpu.roll(stats, head - 2 * heads, 1)
        return stats, weight

    for k, (near, far) in enumerate(((n0, f0), (n1, f1), (n2, f2), (n3, f3))):
        near_level, near_weight = unpack(near)
        far_level, far_weight = unpack(far)
        top = jnp.maximum(near_level, far_level)
        near_scale = jnp.exp2(near_level - top)
        far_scale = jnp.exp2(far_level - top)
        total = near_scale * near_weight + far_scale * far_weight
        near_scale = near_scale / total
        far_scale = far_scale / total
        for h in range(heads):
            place = slice(h * rows, (h + 1) * rows)
            mixed = near[place, :].astype(jnp.float32) * near_scale[:, h : h + 1]
            mixed = mixed + far[place, :].astype(jnp.float32) * far_scale[:, h : h + 1]
            start = pl.multiple_of((member ^ k) * width + h * head, head)
            out[:, pl.ds(start, head)] = mixed.astype(out.dtype)


def merge(heads, near, far, rows):
    head = near[0].shape[1]
    return pl.pallas_call(
        functools.partial(merge_kernel, heads),
        out_shape=jax.ShapeDtypeStruct((rows, GROUP * heads * head), near[0].dtype),
        in_specs=[VMEM] * 8,
        out_specs=VMEM,
        compiler_params=limit(4 * MB),
        cost_estimate=cost(1000),
        name="merge",
    )(*near, *far)


def shards(queries, keys_new, values_new, keys_copy, values_copy, key_bounds, value_bounds):
    rows = queries.shape[0]
    heads = key_bounds.shape[1] // GROUP
    levels = lax.axis_size("patch").bit_length() - 1
    across = 1 << levels - 1
    others = range(1, GROUP)

    far_slab = swapped(queries, across)
    sent = cut(keys_new, values_new, True)
    arrived = [swapped(sent[k - 1], k) for k in others]
    own, old, limits = fetch(
        heads, keys_new, values_new, keys_copy, values_copy, key_bounds, value_bounds
    )
    near = rebuild(heads, own, arrived, old, limits)
    for bit in range(2, levels - 2):
        near = [jnp.concatenate([a, swapped(a, 1 << bit)], axis=0) for a in near]
    far = [swapped(a, 1 << levels - 2) for a in near]
    sent = cut(queries, far_slab, False)
    pieces = [swapped(sent[k - 1], k) for k in others]
    far_out = attend(heads, 1, far_slab, pieces, near, far)
    far_back = [swapped(far_out[k], across + k) for k in range(GROUP)]
    own_out = attend(heads, 0, queries, pieces, near, far)
    own_back = [own_out[0]] + [swapped(own_out[k], k) for k in others]
    return merge(heads, own_back, far_back, rows)


def solution(mesh):
    rows = P(("clips", "patch"), None)
    copies = P(("clips", "patch"), None, None)
    bounds = P("clips", None)
    return jax.shard_map(
        shards,
        mesh=mesh,
        in_specs=(rows, rows, rows, copies, copies, bounds, bounds),
        out_specs=rows,
        check_vma=False,
    )
```

```python
import functools

import jax
import jax.numpy as jnp
from jax import lax
from jax.experimental import pallas as pl
from jax.experimental.pallas import tpu as pltpu
from jax.sharding import PartitionSpec as P

GROUP = 4
LOG2E = 1.4426950408889634
MB = 1 << 20
HBM = pl.BlockSpec(memory_space=pltpu.HBM)
VMEM = pl.BlockSpec(memory_space=pltpu.VMEM)


def limit(size):
    return pltpu.CompilerParams(vmem_limit_bytes=size)


def cost(size):
    return pl.CostEstimate(flops=0, bytes_accessed=size, transcendentals=0)


def swapped(array, mask):
    size = lax.axis_size("patch")
    return lax.ppermute(array, "patch", [(i, i ^ mask) for i in range(size)])


def position():
    place = lax.axis_index("patch")
    return place // GROUP, place % GROUP


def part(index, size):
    return pl.ds(pl.multiple_of(index * size, size), size)


def run_copies(pairs, sems):
    copies = [pltpu.make_async_copy(a, b, sems.at[i]) for i, (a, b) in enumerate(pairs)]
    for copy in copies:
        copy.start()
    for copy in copies:
        copy.wait()


def cut_kernel(count, *refs):
    slabs, sent, kept, sems = refs[:count], refs[-3], refs[-2], refs[-1]
    width = slabs[0].shape[1] // GROUP
    _, member = position()
    pairs = []
    for i, slab in enumerate(slabs):
        for k in range(2):
            pairs.append((slab.at[:, part(member ^ (1 + 2 * k), width)], sent.at[i, k]))
            pairs.append((slab.at[:, part(member ^ (2 * k), width)], kept.at[i, k]))
    run_copies(pairs, sems)


def cut(*slabs):
    rows, features = slabs[0].shape
    shape = jax.ShapeDtypeStruct((len(slabs), 2, rows, features // GROUP), slabs[0].dtype)
    return pl.pallas_call(
        functools.partial(cut_kernel, len(slabs)),
        out_shape=[shape] * 2,
        in_specs=[HBM] * len(slabs),
        out_specs=[VMEM] * 2,
        scratch_shapes=[pltpu.SemaphoreType.DMA((4 * len(slabs),))],
        compiler_params=limit(4 * MB),
        cost_estimate=cost(1000),
        name="cut",
    )(*slabs)


def join_kernel(kept, arrived, keys, values, query, crossing):
    rows = kept.shape[2]
    for i, out in enumerate((keys, values, query)):
        out[:rows] = kept[i, 1]
        out[rows:] = arrived[i, 1]
    for k in range(2):
        crossing[k, :rows] = kept[2, k]
        crossing[k, rows:] = arrived[2, k]


def join(kept, arrived):
    _, _, rows, width = kept.shape
    shape = jax.ShapeDtypeStruct((2 * rows, width), kept.dtype)
    return pl.pallas_call(
        join_kernel,
        out_shape=[shape] * 3 + [jax.ShapeDtypeStruct((2, 2 * rows, width), kept.dtype)],
        in_specs=[VMEM] * 2,
        out_specs=[VMEM] * 4,
        compiler_params=limit(4 * MB),
        cost_estimate=cost(1000),
        name="join",
    )(kept, arrived)


def pair_kernel(query, far_query, *refs):
    out = refs[-1]
    out[0] = query[...]
    out[1] = far_query[1]


def pair(query, far_query, *earlier):
    return pl.pallas_call(
        pair_kernel,
        out_shape=jax.ShapeDtypeStruct(far_query.shape, far_query.dtype),
        in_specs=[VMEM] * 2 + [HBM] * len(earlier),
        out_specs=VMEM,
        compiler_params=limit(4 * MB),
        cost_estimate=cost(1000),
        name="pair",
    )(query, far_query, *earlier)


def fetch_kernel(heads, keys_copy, values_copy, kb, vb, old, limits, lines, turned, sems):
    rows = old.shape[1] // GROUP
    group, member = position()
    block = part(group, GROUP * rows)
    pairs = []
    for i, (copy, bound) in enumerate(((keys_copy, kb), (values_copy, vb))):
        pairs.append((bound.at[:, block], lines.at[i]))
        for k in range(GROUP):
            source = copy.at[0, part(group * GROUP + (member ^ k), rows), :]
            pairs.append((source, old.at[i, pl.ds(k * rows, rows), :]))
    run_copies(pairs, sems)
    for i in range(2):
        chosen = lines[i, pl.ds(member * heads, heads), :]
        padding = jnp.zeros((limits.shape[2] - heads, GROUP * rows), chosen.dtype)
        turned[...] = jnp.concatenate([chosen, padding], axis=0).T
        for k in range(GROUP):
            limits[i, pl.ds(k * rows, rows), :] = turned[part(member ^ k, rows), :]


def fetch(heads, rows, keys_copy, values_copy, key_bounds, value_bounds):
    width = keys_copy.shape[2]
    return pl.pallas_call(
        functools.partial(fetch_kernel, heads),
        out_shape=[
            jax.ShapeDtypeStruct((2, GROUP * rows, width), keys_copy.dtype),
            jax.ShapeDtypeStruct((2, GROUP * rows, 128), key_bounds.dtype),
        ],
        in_specs=[HBM] * 4,
        out_specs=[VMEM] * 2,
        scratch_shapes=[
            pltpu.VMEM((2, key_bounds.shape[1], GROUP * rows), key_bounds.dtype),
            pltpu.VMEM((GROUP * rows, 128), key_bounds.dtype),
            pltpu.SemaphoreType.DMA((10,)),
        ],
        compiler_params=limit(4 * MB),
        cost_estimate=cost(1000),
        name="fetch",
    )(keys_copy, values_copy, key_bounds.T, value_bounds.T)


def rebuild_kernel(heads, i, kept, beside, opposite, old, limits, out):
    rows = kept.shape[2]
    head = kept.shape[3] // heads
    pieces = (kept.at[i, 0], beside.at[i, 0], opposite.at[pl.ds(0, rows)], opposite.at[pl.ds(rows, rows)])
    for k, piece in enumerate(pieces):
        place = slice(k * rows, (k + 1) * rows)
        for h in range(heads):
            lanes = slice(h * head, (h + 1) * head)
            bound = limits[i, place, h : h + 1]
            previous = old[i, place, lanes].astype(jnp.float32)
            change = jnp.clip(piece[:, lanes].astype(jnp.float32) - previous, -bound, bound)
            change = change.astype(jnp.bfloat16).astype(jnp.float32)
            out[place, lanes] = (previous + change).astype(out.dtype)


def rebuild(heads, i, kept, beside, opposite, old, limits):
    return pl.pallas_call(
        functools.partial(rebuild_kernel, heads, i),
        out_shape=jax.ShapeDtypeStruct(old.shape[1:], old.dtype),
        in_specs=[VMEM] * 5,
        out_specs=VMEM,
        compiler_params=limit(4 * MB),
        cost_estimate=cost(1000),
        name="rebuild",
    )(kept, beside, opposite, old, limits)


def attend_kernel(heads, parts, count, *refs):
    queries, (near_keys, near_values, far_keys, far_values) = refs[:count], refs[count : count + 4]
    refs = refs[-len(parts) :]
    width = near_keys.shape[1]
    rows = sum(query.shape[0] for query in queries) // GROUP
    head = width // heads
    outs = [ref.at[j] for ref, group in zip(refs, parts) for j in range(len(group))]
    scale = head ** (-0.5) * LOG2E
    lane = lax.broadcasted_iota(jnp.int32, (GROUP * rows, head), 1)
    stats = jnp.zeros((GROUP * rows, head), jnp.float32)
    contract = (((1,), (1,)), ((), ()))
    for h in range(heads):
        lanes = slice(h * head, (h + 1) * head)
        query = jnp.concatenate([q[:, lanes] for q in queries], axis=0)
        scores = [
            lax.dot_general(query, keys[:, lanes], contract, preferred_element_type=jnp.float32)
            for keys in (near_keys, far_keys)
        ]
        peak = jnp.maximum(
            jnp.max(scores[0], axis=1, keepdims=True), jnp.max(scores[1], axis=1, keepdims=True)
        )
        level = (peak * scale).astype(jnp.bfloat16).astype(jnp.float32)
        total = None
        for values, score in zip((near_values, far_values), scores):
            probs = jnp.exp2(score * scale - level).astype(jnp.bfloat16)
            value = values[:, lanes]
            joined = jnp.concatenate([value, jnp.ones_like(value)], axis=1)
            product = jnp.dot(probs, joined, preferred_element_type=jnp.float32)
            total = product if total is None else total + product
        weighted = total[:, :head].astype(jnp.bfloat16)
        weight = total[:, head:]
        high = weight.astype(jnp.bfloat16).astype(jnp.float32)
        stats = jnp.where(lane == h, level, stats)
        stats = jnp.where(lane == heads + h, high, stats)
        stats = jnp.where(lane == 2 * heads + h, weight - high, stats)
        for k, out in enumerate(outs):
            out[h * rows : (h + 1) * rows, :] = weighted[k * rows : (k + 1) * rows]
    half = rows // 2
    for k, out in enumerate(outs):
        first = stats[k * rows : k * rows + half]
        second = stats[k * rows + half : (k + 1) * rows]
        packed = first + pltpu.roll(second, 16, 1)
        out[heads * rows :, :] = packed.astype(out.dtype)


def far_kernel(heads, parts, far_query, opposite, *refs):
    attend_kernel(heads, parts, 2, far_query.at[0], opposite.at[1], *refs)


def own_kernel(heads, parts, kept, beside, opposite, *refs):
    attend_kernel(heads, parts, 3, kept.at[2, 0], beside.at[2, 0], opposite.at[0], *refs)


def attend(kernel, heads, parts, rows, queries, near, far, *earlier):
    tokens, width = near[0].shape
    shape = (heads * rows + rows // 2, width // heads)
    outs = [jax.ShapeDtypeStruct((len(group),) + shape, near[0].dtype) for group in parts]
    room = 4 * MB + 8 * near[0].size * near[0].dtype.itemsize + 32 * GROUP * rows * tokens
    return pl.pallas_call(
        functools.partial(kernel, heads, parts),
        out_shape=outs,
        in_specs=[VMEM] * (len(queries) + 4) + [HBM] * len(earlier),
        out_specs=[VMEM] * len(outs),
        compiler_params=limit(room),
        cost_estimate=cost(1000),
        name="attend",
    )(*queries, *near, *far, *earlier)


def merge_kernel(heads, n0, n1, n2, n3, f0, f1, f2, f3, out):
    rows = out.shape[0]
    head = n0.shape[2]
    width = heads * head
    _, member = position()

    def unpack(ref):
        packed = ref[0, heads * rows :, :].astype(jnp.float32)
        stats = jnp.concatenate([packed, pltpu.roll(packed, head - 16, 1)], axis=0)
        weight = pltpu.roll(stats, head - heads, 1) + pltpu.roll(stats, head - 2 * heads, 1)
        return stats, weight

    for k, (near, far) in enumerate(((n0, f0), (n1, f1), (n2, f2), (n3, f3))):
        near_level, near_weight = unpack(near)
        far_level, far_weight = unpack(far)
        top = jnp.maximum(near_level, far_level)
        near_scale = jnp.exp2(near_level - top)
        far_scale = jnp.exp2(far_level - top)
        total = near_scale * near_weight + far_scale * far_weight
        near_scale = near_scale / total
        far_scale = far_scale / total
        for h in range(heads):
            place = slice(h * rows, (h + 1) * rows)
            mixed = near[0, place, :].astype(jnp.float32) * near_scale[:, h : h + 1]
            mixed = mixed + far[0, place, :].astype(jnp.float32) * far_scale[:, h : h + 1]
            start = pl.multiple_of((member ^ k) * width + h * head, head)
            out[:, pl.ds(start, head)] = mixed.astype(out.dtype)


def merge(heads, near, far, rows):
    head = near[0].shape[2]
    return pl.pallas_call(
        functools.partial(merge_kernel, heads),
        out_shape=jax.ShapeDtypeStruct((rows, GROUP * heads * head), near[0].dtype),
        in_specs=[VMEM] * 8,
        out_specs=VMEM,
        compiler_params=limit(4 * MB),
        cost_estimate=cost(1000),
        name="merge",
    )(*near, *far)


def shards(queries, keys_new, values_new, keys_copy, values_copy, key_bounds, value_bounds):
    rows = queries.shape[0]
    heads = key_bounds.shape[1] // GROUP
    levels = lax.axis_size("patch").bit_length() - 1
    across = 1 << levels - 1

    pinned = [pltpu.with_memory_space_constraint(a, pltpu.HBM) for a in (keys_new, values_new, queries)]
    copies = [pltpu.with_memory_space_constraint(a, pltpu.HBM) for a in (keys_copy, values_copy)]
    sent, kept = cut(*pinned)
    beside = swapped(sent, 1)
    x_keys, x_values, x_query, crossing = join(kept, beside)
    far_query = swapped(crossing, across)
    opposite = [swapped(a, 2) for a in (x_keys, x_values)]
    old, limits = fetch(heads, rows, *copies, key_bounds, value_bounds)
    near = [rebuild(heads, i, kept, beside, opposite[i], old, limits) for i in range(2)]
    for bit in range(2, levels - 2):
        near = [jnp.concatenate([a, swapped(a, 1 << bit)], axis=0) for a in near]
    far = [swapped(a, 1 << levels - 2) for a in near]
    q_opposite = swapped(pair(x_query, far_query, *near), 2)
    parts = ((0, 1), (2,), (3,))
    far_out = attend(far_kernel, heads, parts, rows, (far_query, q_opposite), near, far)
    f01, f2, f3 = [swapped(a, across + group[0]) for a, group in zip(far_out, parts)]
    parts = ((0,), (1,), (2, 3))
    own_query = (kept, beside, q_opposite)
    n0, n1, n23 = attend(own_kernel, heads, parts, rows, own_query, near, far, far_out[2])
    n1, n23 = swapped(n1, 1), swapped(n23, 2)
    near_parts = (n0, n1, n23, swapped(n23[1:], 1))
    far_parts = (f01, swapped(f01[1:], 1), f2, f3)
    return merge(heads, near_parts, far_parts, rows)


def solution(mesh):
    rows = P(("clips", "patch"), None)
    copies = P(("clips", "patch"), None, None)
    bounds = P("clips", None)
    return jax.shard_map(
        shards,
        mesh=mesh,
        in_specs=(rows, rows, rows, copies, copies, bounds, bounds),
        out_specs=rows,
        check_vma=False,
    )
```

```python
import functools

import jax
import jax.numpy as jnp
from jax import lax
from jax.experimental import pallas as pl
from jax.experimental.pallas import tpu as pltpu
from jax.sharding import PartitionSpec as P

GROUP = 4
LOG2E = 1.4426950408889634
MB = 1 << 20
HBM = pl.BlockSpec(memory_space=pltpu.HBM)
VMEM = pl.BlockSpec(memory_space=pltpu.VMEM)


def limit(size):
    return pltpu.CompilerParams(vmem_limit_bytes=size)


def cost(size):
    return pl.CostEstimate(flops=0, bytes_accessed=size, transcendentals=0)


def swapped(array, mask):
    size = lax.axis_size("patch")
    return lax.ppermute(array, "patch", [(i, i ^ mask) for i in range(size)])


def position():
    place = lax.axis_index("patch")
    return place // GROUP, place % GROUP


def part(index, size):
    return pl.ds(pl.multiple_of(index * size, size), size)


def run_copies(pairs, sems):
    copies = [pltpu.make_async_copy(a, b, sems.at[i]) for i, (a, b) in enumerate(pairs)]
    for copy in copies:
        copy.start()
    for copy in copies:
        copy.wait()


def cut_kernel(count, *refs):
    slabs, sent, kept, sems = refs[:count], refs[-3], refs[-2], refs[-1]
    width = slabs[0].shape[1] // GROUP
    _, member = position()
    pairs = []
    for i, slab in enumerate(slabs):
        for k in range(2):
            pairs.append((slab.at[:, part(member ^ (1 + 2 * k), width)], sent.at[i, k]))
            pairs.append((slab.at[:, part(member ^ (2 * k), width)], kept.at[i, k]))
    run_copies(pairs, sems)


def cut(*slabs):
    rows, features = slabs[0].shape
    shape = jax.ShapeDtypeStruct((len(slabs), 2, rows, features // GROUP), slabs[0].dtype)
    return pl.pallas_call(
        functools.partial(cut_kernel, len(slabs)),
        out_shape=[shape] * 2,
        in_specs=[HBM] * len(slabs),
        out_specs=[VMEM] * 2,
        scratch_shapes=[pltpu.SemaphoreType.DMA((4 * len(slabs),))],
        compiler_params=limit(4 * MB),
        cost_estimate=cost(1000),
        name="cut",
    )(*slabs)


def join_kernel(kept, arrived, keys, values, query, crossing):
    rows = kept.shape[2]
    for i, out in enumerate((keys, values, query)):
        out[:rows] = kept[i, 1]
        out[rows:] = arrived[i, 1]
    for k in range(2):
        crossing[k, :rows] = kept[2, k]
        crossing[k, rows:] = arrived[2, k]


def join(kept, arrived):
    _, _, rows, width = kept.shape
    shape = jax.ShapeDtypeStruct((2 * rows, width), kept.dtype)
    return pl.pallas_call(
        join_kernel,
        out_shape=[shape] * 3 + [jax.ShapeDtypeStruct((2, 2 * rows, width), kept.dtype)],
        in_specs=[VMEM] * 2,
        out_specs=[VMEM] * 4,
        compiler_params=limit(4 * MB),
        cost_estimate=cost(1000),
        name="join",
    )(kept, arrived)


def pair_kernel(query, far_query, *refs):
    out = refs[-1]
    out[0] = query[...]
    out[1] = far_query[1]


def pair(query, far_query, *earlier):
    return pl.pallas_call(
        pair_kernel,
        out_shape=jax.ShapeDtypeStruct(far_query.shape, far_query.dtype),
        in_specs=[VMEM] * 2 + [HBM] * len(earlier),
        out_specs=VMEM,
        compiler_params=limit(4 * MB),
        cost_estimate=cost(1000),
        name="pair",
    )(query, far_query, *earlier)


def fetch_kernel(heads, keys_copy, values_copy, kb, vb, old, limits, lines, turned, sems):
    rows = old.shape[1] // GROUP
    group, member = position()
    block = part(group, GROUP * rows)
    pairs = []
    for i, (copy, bound) in enumerate(((keys_copy, kb), (values_copy, vb))):
        pairs.append((bound.at[:, block], lines.at[i]))
        for k in range(GROUP):
            source = copy.at[0, part(group * GROUP + (member ^ k), rows), :]
            pairs.append((source, old.at[i, pl.ds(k * rows, rows), :]))
    run_copies(pairs, sems)
    for i in range(2):
        chosen = lines[i, pl.ds(member * heads, heads), :]
        padding = jnp.zeros((limits.shape[2] - heads, GROUP * rows), chosen.dtype)
        turned[...] = jnp.concatenate([chosen, padding], axis=0).T
        for k in range(GROUP):
            limits[i, pl.ds(k * rows, rows), :] = turned[part(member ^ k, rows), :]


def fetch(heads, rows, keys_copy, values_copy, key_bounds, value_bounds):
    width = keys_copy.shape[2]
    return pl.pallas_call(
        functools.partial(fetch_kernel, heads),
        out_shape=[
            jax.ShapeDtypeStruct((2, GROUP * rows, width), keys_copy.dtype),
            jax.ShapeDtypeStruct((2, GROUP * rows, 128), key_bounds.dtype),
        ],
        in_specs=[HBM] * 4,
        out_specs=[VMEM] * 2,
        scratch_shapes=[
            pltpu.VMEM((2, key_bounds.shape[1], GROUP * rows), key_bounds.dtype),
            pltpu.VMEM((GROUP * rows, 128), key_bounds.dtype),
            pltpu.SemaphoreType.DMA((10,)),
        ],
        compiler_params=limit(4 * MB),
        cost_estimate=cost(1000),
        name="fetch",
    )(keys_copy, values_copy, key_bounds.T, value_bounds.T)


def rebuild_kernel(heads, i, kept, beside, opposite, old, limits, out):
    rows = kept.shape[2]
    head = kept.shape[3] // heads
    pieces = (kept.at[i, 0], beside.at[i, 0], opposite.at[pl.ds(0, rows)], opposite.at[pl.ds(rows, rows)])
    for k, piece in enumerate(pieces):
        place = slice(k * rows, (k + 1) * rows)
        for h in range(heads):
            lanes = slice(h * head, (h + 1) * head)
            bound = limits[i, place, h : h + 1]
            previous = old[i, place, lanes].astype(jnp.float32)
            change = jnp.clip(piece[:, lanes].astype(jnp.float32) - previous, -bound, bound)
            change = change.astype(jnp.bfloat16).astype(jnp.float32)
            out[place, lanes] = (previous + change).astype(out.dtype)


def rebuild(heads, i, kept, beside, opposite, old, limits):
    return pl.pallas_call(
        functools.partial(rebuild_kernel, heads, i),
        out_shape=jax.ShapeDtypeStruct(old.shape[1:], old.dtype),
        in_specs=[VMEM] * 5,
        out_specs=VMEM,
        compiler_params=limit(4 * MB),
        cost_estimate=cost(1000),
        name="rebuild",
    )(kept, beside, opposite, old, limits)


def attend_kernel(heads, parts, count, *refs):
    queries, (near_keys, near_values, far_keys, far_values) = refs[:count], refs[count : count + 4]
    refs = refs[-len(parts) :]
    width = near_keys.shape[1]
    rows = sum(query.shape[0] for query in queries) // GROUP
    head = width // heads
    outs = {k: ref.at[j] for ref, group in zip(refs, parts) for j, k in enumerate(group)}
    scale = head ** (-0.5) * LOG2E
    lane = lax.broadcasted_iota(jnp.int32, (GROUP * rows, head), 1)
    stats = jnp.zeros((GROUP * rows, head), jnp.float32)
    contract = (((1,), (1,)), ((), ()))
    for h in range(heads):
        lanes = slice(h * head, (h + 1) * head)
        query = jnp.concatenate([q[:, lanes] for q in queries], axis=0)
        scores = [
            lax.dot_general(query, keys[:, lanes], contract, preferred_element_type=jnp.float32)
            for keys in (near_keys, far_keys)
        ]
        peak = jnp.maximum(
            jnp.max(scores[0], axis=1, keepdims=True), jnp.max(scores[1], axis=1, keepdims=True)
        )
        level = (peak * scale).astype(jnp.bfloat16).astype(jnp.float32)
        total = None
        for values, score in zip((near_values, far_values), scores):
            probs = jnp.exp2(score * scale - level).astype(jnp.bfloat16)
            value = values[:, lanes]
            joined = jnp.concatenate([value, jnp.ones_like(value)], axis=1)
            product = jnp.dot(probs, joined, preferred_element_type=jnp.float32)
            total = product if total is None else total + product
        weighted = total[:, :head].astype(jnp.bfloat16)
        weight = total[:, head:]
        high = weight.astype(jnp.bfloat16).astype(jnp.float32)
        stats = jnp.where(lane == h, level, stats)
        stats = jnp.where(lane == heads + h, high, stats)
        stats = jnp.where(lane == 2 * heads + h, weight - high, stats)
        for k, out in sorted(outs.items()):
            out[h * rows : (h + 1) * rows, :] = weighted[k * rows : (k + 1) * rows]
    half = rows // 2
    for k, out in sorted(outs.items()):
        first = stats[k * rows : k * rows + half]
        second = stats[k * rows + half : (k + 1) * rows]
        packed = first + pltpu.roll(second, 16, 1)
        out[heads * rows :, :] = packed.astype(out.dtype)


def far_kernel(heads, parts, far_query, opposite, *refs):
    attend_kernel(heads, parts, 2, far_query.at[0], opposite.at[1], *refs)


def own_kernel(heads, parts, kept, beside, opposite, *refs):
    attend_kernel(heads, parts, 3, kept.at[2, 0], beside.at[2, 0], opposite.at[0], *refs)


def attend(kernel, heads, parts, rows, queries, near, far, *earlier):
    tokens, width = near[0].shape
    shape = (heads * rows + rows // 2, width // heads)
    outs = [jax.ShapeDtypeStruct((len(group),) + shape, near[0].dtype) for group in parts]
    room = 4 * MB + 8 * near[0].size * near[0].dtype.itemsize + 32 * GROUP * rows * tokens
    return pl.pallas_call(
        functools.partial(kernel, heads, parts),
        out_shape=outs,
        in_specs=[VMEM] * (len(queries) + 4) + [HBM] * len(earlier),
        out_specs=[VMEM] * len(outs),
        compiler_params=limit(room),
        cost_estimate=cost(1000),
        name="attend",
    )(*queries, *near, *far, *earlier)


def merge_kernel(heads, n0, n1, n2, n3, f0, f1, f2, f3, out):
    rows = out.shape[0]
    head = n0.shape[2]
    width = heads * head
    _, member = position()

    def unpack(ref):
        packed = ref[0, heads * rows :, :].astype(jnp.float32)
        stats = jnp.concatenate([packed, pltpu.roll(packed, head - 16, 1)], axis=0)
        weight = pltpu.roll(stats, head - heads, 1) + pltpu.roll(stats, head - 2 * heads, 1)
        return stats, weight

    for k, (near, far) in enumerate(((n0, f0), (n1, f1), (n2, f2), (n3, f3))):
        near_level, near_weight = unpack(near)
        far_level, far_weight = unpack(far)
        top = jnp.maximum(near_level, far_level)
        near_scale = jnp.exp2(near_level - top)
        far_scale = jnp.exp2(far_level - top)
        total = near_scale * near_weight + far_scale * far_weight
        near_scale = near_scale / total
        far_scale = far_scale / total
        for h in range(heads):
            place = slice(h * rows, (h + 1) * rows)
            mixed = near[0, place, :].astype(jnp.float32) * near_scale[:, h : h + 1]
            mixed = mixed + far[0, place, :].astype(jnp.float32) * far_scale[:, h : h + 1]
            start = pl.multiple_of((member ^ k) * width + h * head, head)
            out[:, pl.ds(start, head)] = mixed.astype(out.dtype)


def merge(heads, near, far, rows):
    head = near[0].shape[2]
    return pl.pallas_call(
        functools.partial(merge_kernel, heads),
        out_shape=jax.ShapeDtypeStruct((rows, GROUP * heads * head), near[0].dtype),
        in_specs=[VMEM] * 8,
        out_specs=VMEM,
        compiler_params=limit(4 * MB),
        cost_estimate=cost(1000),
        name="merge",
    )(*near, *far)


def shards(queries, keys_new, values_new, keys_copy, values_copy, key_bounds, value_bounds):
    rows = queries.shape[0]
    heads = key_bounds.shape[1] // GROUP
    levels = lax.axis_size("patch").bit_length() - 1
    across = 1 << levels - 1

    pinned = [pltpu.with_memory_space_constraint(a, pltpu.HBM) for a in (keys_new, values_new, queries)]
    copies = [pltpu.with_memory_space_constraint(a, pltpu.HBM) for a in (keys_copy, values_copy)]
    sent, kept = cut(*pinned)
    beside = swapped(sent, 1)
    x_keys, x_values, x_query, crossing = join(kept, beside)
    far_query = swapped(crossing, across)
    opposite = [swapped(a, 2) for a in (x_keys, x_values)]
    old, limits = fetch(heads, rows, *copies, key_bounds, value_bounds)
    near = [rebuild(heads, i, kept, beside, opposite[i], old, limits) for i in range(2)]
    for bit in range(2, levels - 2):
        near = [jnp.concatenate([a, swapped(a, 1 << bit)], axis=0) for a in near]
    far = [swapped(a, 1 << levels - 2) for a in near]
    q_opposite = swapped(pair(x_query, far_query, *near), 2)
    parts = ((2, 3), (0,), (1,))
    far_out = attend(far_kernel, heads, parts, rows, (far_query, q_opposite), near, far)
    f23, f0, f1 = [swapped(a, across + group[0]) for a, group in zip(far_out, parts)]
    parts = ((0,), (1,), (2, 3))
    own_query = (kept, beside, q_opposite)
    n0, n1, n23 = attend(own_kernel, heads, parts, rows, own_query, near, far, far_out[2])
    n1, n23 = swapped(n1, 1), swapped(n23, 2)
    near_parts = (n0, n1, n23, swapped(n23[1:], 1))
    far_parts = (f0, f1, f23, swapped(f23[1:], 1))
    return merge(heads, near_parts, far_parts, rows)


def solution(mesh):
    rows = P(("clips", "patch"), None)
    copies = P(("clips", "patch"), None, None)
    bounds = P("clips", None)
    return jax.shard_map(
        shards,
        mesh=mesh,
        in_specs=(rows, rows, rows, copies, copies, bounds, bounds),
        out_specs=rows,
        check_vma=False,
    )
```

```python
import functools

import jax
import jax.numpy as jnp
from jax import lax
from jax.experimental import pallas as pl
from jax.experimental.pallas import tpu as pltpu
from jax.sharding import PartitionSpec as P

GROUP = 4
LOG2E = 1.4426950408889634
MB = 1 << 20
HBM = pl.BlockSpec(memory_space=pltpu.HBM)
VMEM = pl.BlockSpec(memory_space=pltpu.VMEM)


def limit(size):
    return pltpu.CompilerParams(vmem_limit_bytes=size)


def cost(size):
    return pl.CostEstimate(flops=0, bytes_accessed=size, transcendentals=0)


def swapped(array, mask):
    size = lax.axis_size("patch")
    return lax.ppermute(array, "patch", [(i, i ^ mask) for i in range(size)])


def position():
    place = lax.axis_index("patch")
    return place // GROUP, place % GROUP


def part(index, size):
    return pl.ds(pl.multiple_of(index * size, size), size)


def run_copies(pairs, sems):
    copies = [pltpu.make_async_copy(a, b, sems.at[i]) for i, (a, b) in enumerate(pairs)]
    for copy in copies:
        copy.start()
    for copy in copies:
        copy.wait()


def cut_kernel(count, *refs):
    slabs, sent, kept, sems = refs[:count], refs[-3], refs[-2], refs[-1]
    width = slabs[0].shape[1] // GROUP
    _, member = position()
    pairs = []
    for i, slab in enumerate(slabs):
        for k in range(2):
            pairs.append((slab.at[:, part(member ^ (1 + 2 * k), width)], sent.at[i, k]))
            pairs.append((slab.at[:, part(member ^ (2 * k), width)], kept.at[i, k]))
    run_copies(pairs, sems)


def cut(*slabs):
    rows, features = slabs[0].shape
    shape = jax.ShapeDtypeStruct((len(slabs), 2, rows, features // GROUP), slabs[0].dtype)
    return pl.pallas_call(
        functools.partial(cut_kernel, len(slabs)),
        out_shape=[shape] * 2,
        in_specs=[HBM] * len(slabs),
        out_specs=[VMEM] * 2,
        scratch_shapes=[pltpu.SemaphoreType.DMA((4 * len(slabs),))],
        compiler_params=limit(4 * MB),
        cost_estimate=cost(1000),
        name="cut",
    )(*slabs)


def join_kernel(kept, arrived, x_query, x_keys, x_values, z_values):
    rows = kept.shape[2]
    for i, out in ((0, x_keys), (1, x_values), (2, x_query)):
        out[:rows] = kept[i, 1]
        out[rows:] = arrived[i, 1]
    for k in range(2):
        z_values[k, :rows] = kept[1, k]
        z_values[k, rows:] = arrived[1, k]


def join(kept, arrived):
    _, _, rows, width = kept.shape
    shape = (2 * rows, width)
    return pl.pallas_call(
        join_kernel,
        out_shape=[jax.ShapeDtypeStruct(shape, kept.dtype)] * 3 + [jax.ShapeDtypeStruct((2,) + shape, kept.dtype)],
        in_specs=[VMEM] * 2,
        out_specs=[VMEM] * 4,
        compiler_params=limit(4 * MB),
        cost_estimate=cost(1000),
        name="join",
    )(kept, arrived)


def assemble_kernel(kept, beside, opposite, out):
    rows = kept.shape[2]
    out[:rows] = kept[2, 0]
    out[rows : 2 * rows] = beside[2, 0]
    out[2 * rows :] = opposite[...]


def assemble(kept, beside, opposite):
    _, _, rows, width = kept.shape
    return pl.pallas_call(
        assemble_kernel,
        out_shape=jax.ShapeDtypeStruct((GROUP * rows, width), kept.dtype),
        in_specs=[VMEM] * 3,
        out_specs=VMEM,
        compiler_params=limit(4 * MB),
        cost_estimate=cost(1000),
        name="assemble",
    )(kept, beside, opposite)


def pick_kernel(both, *refs):
    refs[-1][...] = both[1]


def pick(both, *earlier):
    return pl.pallas_call(
        pick_kernel,
        out_shape=jax.ShapeDtypeStruct(both.shape[1:], both.dtype),
        in_specs=[VMEM] + [HBM] * len(earlier),
        out_specs=VMEM,
        compiler_params=limit(4 * MB + 2 * both.size * both.dtype.itemsize),
        cost_estimate=cost(1000),
        name="pick",
    )(both, *earlier)


def fetch_kernel(heads, count, keys_copy, values_copy, kb, vb, old, limits, lines, turned, sems):
    rows = old.shape[1] // GROUP
    group, member = position()
    sources = [(keys_copy, kb, group)] + [(values_copy, vb, group ^ j) for j in range(count)]
    pairs = []
    for i, (copy, bound, block) in enumerate(sources):
        pairs.append((bound.at[:, part(block, GROUP * rows)], lines.at[i]))
        for k in range(GROUP):
            source = copy.at[0, part(block * GROUP + (member ^ k), rows), :]
            pairs.append((source, old.at[i, pl.ds(k * rows, rows), :]))
    run_copies(pairs, sems)
    for i in range(len(sources)):
        chosen = lines[i, pl.ds(member * heads, heads), :]
        padding = jnp.zeros((limits.shape[2] - heads, GROUP * rows), chosen.dtype)
        turned[...] = jnp.concatenate([chosen, padding], axis=0).T
        for k in range(GROUP):
            limits[i, pl.ds(k * rows, rows), :] = turned[part(member ^ k, rows), :]


def fetch(heads, rows, count, keys_copy, values_copy, key_bounds, value_bounds):
    width = keys_copy.shape[2]
    return pl.pallas_call(
        functools.partial(fetch_kernel, heads, count),
        out_shape=[
            jax.ShapeDtypeStruct((1 + count, GROUP * rows, width), keys_copy.dtype),
            jax.ShapeDtypeStruct((1 + count, GROUP * rows, 128), key_bounds.dtype),
        ],
        in_specs=[HBM] * 4,
        out_specs=[VMEM] * 2,
        scratch_shapes=[
            pltpu.VMEM((1 + count, key_bounds.shape[1], GROUP * rows), key_bounds.dtype),
            pltpu.VMEM((GROUP * rows, 128), key_bounds.dtype),
            pltpu.SemaphoreType.DMA(((1 + GROUP) * (1 + count),)),
        ],
        compiler_params=limit(4 * MB + MB * count),
        cost_estimate=cost(1000),
        name="fetch",
    )(keys_copy, values_copy, key_bounds.T, value_bounds.T)


def restore(heads, pieces, old, limits, out, start):
    rows, width = pieces[0].shape
    head = width // heads
    for k, piece in enumerate(pieces):
        place = slice(k * rows, (k + 1) * rows)
        for h in range(heads):
            lanes = slice(h * head, (h + 1) * head)
            bound = limits[place, h : h + 1]
            previous = old[place, lanes].astype(jnp.float32)
            change = jnp.clip(piece[:, lanes].astype(jnp.float32) - previous, -bound, bound)
            change = change.astype(jnp.bfloat16).astype(jnp.float32)
            out[start + k * rows : start + (k + 1) * rows, lanes] = (previous + change).astype(out.dtype)


def rebuild_keys_kernel(heads, kept, beside, opposite, old, limits, _, out):
    rows = kept.shape[2]
    pieces = [kept.at[0, 0], beside.at[0, 0], opposite.at[pl.ds(0, rows)], opposite.at[pl.ds(rows, rows)]]
    restore(heads, pieces, old.at[0], limits.at[0], out, 0)


def rebuild_values_kernel(heads, first, this, opposite, old, limits, *refs):
    out = refs[-1]
    rows = old.shape[1] // GROUP
    for j in range(this.shape[1] // (2 * rows)):
        starts = [2 * j * rows, (2 * j + 1) * rows]
        pieces = [this.at[0, pl.ds(start, rows)] for start in starts]
        pieces += [opposite.at[pl.ds(start, rows)] for start in starts]
        restore(heads, pieces, old.at[1 + first + j], limits.at[1 + first + j], out, j * GROUP * rows)


def rebuild(kernel, tokens, old, *operands):
    return pl.pallas_call(
        kernel,
        out_shape=jax.ShapeDtypeStruct((tokens, old.shape[2]), old.dtype),
        in_specs=[VMEM] * len(operands),
        out_specs=VMEM,
        compiler_params=limit(4 * MB + 16 * tokens * old.shape[2]),
        cost_estimate=cost(1000),
        name="rebuild",
    )(*operands)


def attend_kernel(heads, parts, query_ref, near_keys, near_values, far_keys, far_values, *refs):
    refs = refs[-len(parts) :]
    width = near_keys.shape[1]
    rows = query_ref.shape[0] // GROUP
    head = width // heads
    outs = {k: ref.at[j] for ref, group in zip(refs, parts) for j, k in enumerate(group)}
    scale = head ** (-0.5) * LOG2E
    lane = lax.broadcasted_iota(jnp.int32, (GROUP * rows, head), 1)
    stats = jnp.zeros((GROUP * rows, head), jnp.float32)
    contract = (((1,), (1,)), ((), ()))
    for h in range(heads):
        lanes = slice(h * head, (h + 1) * head)
        query = query_ref[:, lanes]
        scores = [
            lax.dot_general(query, keys[:, lanes], contract, preferred_element_type=jnp.float32)
            for keys in (near_keys, far_keys)
        ]
        peak = jnp.maximum(
            jnp.max(scores[0], axis=1, keepdims=True), jnp.max(scores[1], axis=1, keepdims=True)
        )
        level = (peak * scale).astype(jnp.bfloat16).astype(jnp.float32)
        total = None
        for values, score in zip((near_values, far_values), scores):
            probs = jnp.exp2(score * scale - level).astype(jnp.bfloat16)
            value = values[:, lanes]
            joined = jnp.concatenate([value, jnp.ones_like(value)], axis=1)
            product = jnp.dot(probs, joined, preferred_element_type=jnp.float32)
            total = product if total is None else total + product
        weighted = total[:, :head].astype(jnp.bfloat16)
        weight = total[:, head:]
        high = weight.astype(jnp.bfloat16).astype(jnp.float32)
        stats = jnp.where(lane == h, level, stats)
        stats = jnp.where(lane == heads + h, high, stats)
        stats = jnp.where(lane == 2 * heads + h, weight - high, stats)
        for k, out in sorted(outs.items()):
            out[h * rows : (h + 1) * rows, :] = weighted[k * rows : (k + 1) * rows]
    half = rows // 2
    for k, out in sorted(outs.items()):
        first = stats[k * rows : k * rows + half]
        second = stats[k * rows + half : (k + 1) * rows]
        packed = first + pltpu.roll(second, 16, 1)
        out[heads * rows :, :] = packed.astype(out.dtype)


def attend(heads, parts, query, near, far, *earlier):
    tokens, width = near[0].shape
    rows = query.shape[0] // GROUP
    shape = (heads * rows + rows // 2, width // heads)
    outs = [jax.ShapeDtypeStruct((len(group),) + shape, near[0].dtype) for group in parts]
    room = 4 * MB + 8 * near[0].size * near[0].dtype.itemsize + 32 * GROUP * rows * tokens
    return pl.pallas_call(
        functools.partial(attend_kernel, heads, parts),
        out_shape=outs,
        in_specs=[VMEM] * 5 + [HBM] * len(earlier),
        out_specs=[VMEM] * len(outs),
        compiler_params=limit(room),
        cost_estimate=cost(1000),
        name="attend",
    )(query, *near, *far, *earlier)


def merge_kernel(heads, n0, n1, n2, n3, f0, f1, f2, f3, out):
    rows = out.shape[0]
    head = n0.shape[2]
    width = heads * head
    _, member = position()

    def unpack(ref):
        packed = ref[0, heads * rows :, :].astype(jnp.float32)
        stats = jnp.concatenate([packed, pltpu.roll(packed, head - 16, 1)], axis=0)
        weight = pltpu.roll(stats, head - heads, 1) + pltpu.roll(stats, head - 2 * heads, 1)
        return stats, weight

    for k, (near, far) in enumerate(((n0, f0), (n1, f1), (n2, f2), (n3, f3))):
        near_level, near_weight = unpack(near)
        far_level, far_weight = unpack(far)
        top = jnp.maximum(near_level, far_level)
        near_scale = jnp.exp2(near_level - top)
        far_scale = jnp.exp2(far_level - top)
        total = near_scale * near_weight + far_scale * far_weight
        near_scale = near_scale / total
        far_scale = far_scale / total
        for h in range(heads):
            place = slice(h * rows, (h + 1) * rows)
            mixed = near[0, place, :].astype(jnp.float32) * near_scale[:, h : h + 1]
            mixed = mixed + far[0, place, :].astype(jnp.float32) * far_scale[:, h : h + 1]
            start = pl.multiple_of((member ^ k) * width + h * head, head)
            out[:, pl.ds(start, head)] = mixed.astype(out.dtype)


def merge(heads, near, far, rows):
    head = near[0].shape[2]
    return pl.pallas_call(
        functools.partial(merge_kernel, heads),
        out_shape=jax.ShapeDtypeStruct((rows, GROUP * heads * head), near[0].dtype),
        in_specs=[VMEM] * 8,
        out_specs=VMEM,
        compiler_params=limit(4 * MB),
        cost_estimate=cost(1000),
        name="merge",
    )(*near, *far)


def shards(queries, keys_new, values_new, keys_copy, values_copy, key_bounds, value_bounds):
    rows = queries.shape[0]
    heads = key_bounds.shape[1] // GROUP
    levels = lax.axis_size("patch").bit_length() - 1
    across = 1 << levels - 1

    pinned = [pltpu.with_memory_space_constraint(a, pltpu.HBM) for a in (keys_new, values_new, queries)]
    copies = [pltpu.with_memory_space_constraint(a, pltpu.HBM) for a in (keys_copy, values_copy)]
    sent, kept = cut(*pinned)
    beside = swapped(sent, 1)
    x_query, x_keys, x_own, near_raw = join(kept, beside)
    own_query = assemble(kept, beside, swapped(x_query, 2))
    far_query = swapped(own_query, across)
    bits = [1 << bit for bit in range(2, levels - 1)]
    for bit in bits[:-1]:
        near_raw = jnp.concatenate([near_raw, swapped(near_raw, bit)], axis=1)
    far_raw = swapped(near_raw, bits[-1])
    if len(bits) > 1:
        x_own = near_raw[1]
    x_keys, x_own = swapped(x_keys, 2), swapped(x_own, 2)
    count = 1 << len(bits)
    old, limits = fetch(heads, rows, count, *copies, key_bounds, value_bounds)
    block = GROUP * rows
    rebuild_keys = functools.partial(rebuild_keys_kernel, heads)
    near_keys = rebuild(rebuild_keys, block, old, kept, beside, x_keys, old, limits, own_query)
    picked = pick(far_raw, near_keys)
    for bit in bits[:-1]:
        near_keys = jnp.concatenate([near_keys, swapped(near_keys, bit)], axis=0)
    far_keys = swapped(near_keys, bits[-1])
    halves = []
    sides = ((0, near_raw, x_own, own_query), (count // 2, far_raw, swapped(picked, 2), far_query))
    for first, this, opposite, earlier in sides:
        kernel = functools.partial(rebuild_values_kernel, heads, first)
        halves.append(rebuild(kernel, block * count // 2, old, this, opposite, old, limits, earlier))
    near, far = (near_keys, halves[0]), (far_keys, halves[1])
    parts = ((2, 3), (0,), (1,))
    far_out = attend(heads, parts, far_query, near, far)
    f23, f0, f1 = [swapped(a, across + group[0]) for a, group in zip(far_out, parts)]
    parts = ((0,), (1,), (2, 3))
    n0, n1, n23 = attend(heads, parts, own_query, near, far, far_out[2])
    n1, n23 = swapped(n1, 1), swapped(n23, 2)
    f3 = pick(f23)
    n3 = pick(n23, f3)
    near_parts = (n0, n1, n23, swapped(n3, 1)[None])
    far_parts = (f0, f1, f23, swapped(f3, 1)[None])
    return merge(heads, near_parts, far_parts, rows)


def solution(mesh):
    rows = P(("clips", "patch"), None)
    copies = P(("clips", "patch"), None, None)
    bounds = P("clips", None)
    return jax.shard_map(
        shards,
        mesh=mesh,
        in_specs=(rows, rows, rows, copies, copies, bounds, bounds),
        out_specs=rows,
        check_vma=False,
    )
```

```python
import functools

import jax
import jax.numpy as jnp
from jax import lax
from jax.experimental import pallas as pl
from jax.experimental.pallas import tpu as pltpu
from jax.sharding import PartitionSpec as P

GROUP = 4
LOG2E = 1.4426950408889634
MB = 1 << 20
HBM = pl.BlockSpec(memory_space=pltpu.HBM)
VMEM = pl.BlockSpec(memory_space=pltpu.VMEM)


def limit(size):
    return pltpu.CompilerParams(vmem_limit_bytes=size)


def cost(size):
    return pl.CostEstimate(flops=0, bytes_accessed=size, transcendentals=0)


def swapped(array, mask):
    size = lax.axis_size("patch")
    return lax.ppermute(array, "patch", [(i, i ^ mask) for i in range(size)])


def position():
    place = lax.axis_index("patch")
    return place // GROUP, place % GROUP


def part(index, size):
    return pl.ds(pl.multiple_of(index * size, size), size)


def run_copies(pairs, sems):
    copies = [pltpu.make_async_copy(a, b, sems.at[i]) for i, (a, b) in enumerate(pairs)]
    for copy in copies:
        copy.start()
    for copy in copies:
        copy.wait()


def cut_kernel(count, *refs):
    slabs, sent, kept, sems = refs[:count], refs[-3], refs[-2], refs[-1]
    width = slabs[0].shape[1] // GROUP
    _, member = position()
    pairs = []
    for i, slab in enumerate(slabs):
        for k in range(2):
            pairs.append((slab.at[:, part(member ^ (1 + 2 * k), width)], sent.at[i, k]))
            pairs.append((slab.at[:, part(member ^ (2 * k), width)], kept.at[i, k]))
    run_copies(pairs, sems)


def cut(*slabs):
    rows, features = slabs[0].shape
    shape = jax.ShapeDtypeStruct((len(slabs), 2, rows, features // GROUP), slabs[0].dtype)
    return pl.pallas_call(
        functools.partial(cut_kernel, len(slabs)),
        out_shape=[shape] * 2,
        in_specs=[HBM] * len(slabs),
        out_specs=[VMEM] * 2,
        scratch_shapes=[pltpu.SemaphoreType.DMA((4 * len(slabs),))],
        compiler_params=limit(4 * MB),
        cost_estimate=cost(1000),
        name="cut",
    )(*slabs)


def join_kernel(kept, arrived, x_query, x_keys, x_values, z_values):
    rows = kept.shape[2]
    for i, out in ((0, x_keys), (1, x_values), (2, x_query)):
        out[:rows] = kept[i, 1]
        out[rows:] = arrived[i, 1]
    for k in range(2):
        z_values[k, :rows] = kept[1, k]
        z_values[k, rows:] = arrived[1, k]


def join(kept, arrived):
    _, _, rows, width = kept.shape
    shape = (2 * rows, width)
    return pl.pallas_call(
        join_kernel,
        out_shape=[jax.ShapeDtypeStruct(shape, kept.dtype)] * 3 + [jax.ShapeDtypeStruct((2,) + shape, kept.dtype)],
        in_specs=[VMEM] * 2,
        out_specs=[VMEM] * 4,
        compiler_params=limit(4 * MB),
        cost_estimate=cost(1000),
        name="join",
    )(kept, arrived)


def assemble_kernel(kept, beside, opposite, out):
    rows = kept.shape[2]
    out[:rows] = kept[2, 0]
    out[rows : 2 * rows] = beside[2, 0]
    out[2 * rows :] = opposite[...]


def assemble(kept, beside, opposite):
    _, _, rows, width = kept.shape
    return pl.pallas_call(
        assemble_kernel,
        out_shape=jax.ShapeDtypeStruct((GROUP * rows, width), kept.dtype),
        in_specs=[VMEM] * 3,
        out_specs=VMEM,
        compiler_params=limit(4 * MB),
        cost_estimate=cost(1000),
        name="assemble",
    )(kept, beside, opposite)


def pick_kernel(both, *refs):
    refs[-1][...] = both[1]


def pick(both, *earlier):
    return pl.pallas_call(
        pick_kernel,
        out_shape=jax.ShapeDtypeStruct(both.shape[1:], both.dtype),
        in_specs=[VMEM] + [HBM] * len(earlier),
        out_specs=VMEM,
        compiler_params=limit(4 * MB + 2 * both.size * both.dtype.itemsize),
        cost_estimate=cost(4_000_000),
        name="pick",
    )(both, *earlier)


def fetch_kernel(heads, count, keys_copy, values_copy, kb, vb, old, limits, lines, turned, sems):
    rows = old.shape[1] // GROUP
    group, member = position()
    sources = [(keys_copy, kb, group)] + [(values_copy, vb, group ^ j) for j in range(count)]
    pairs = []
    for i, (copy, bound, block) in enumerate(sources):
        pairs.append((bound.at[:, part(block, GROUP * rows)], lines.at[i]))
        for k in range(GROUP):
            source = copy.at[0, part(block * GROUP + (member ^ k), rows), :]
            pairs.append((source, old.at[i, pl.ds(k * rows, rows), :]))
    run_copies(pairs, sems)
    for i in range(len(sources)):
        chosen = lines[i, pl.ds(member * heads, heads), :]
        padding = jnp.zeros((limits.shape[2] - heads, GROUP * rows), chosen.dtype)
        turned[...] = jnp.concatenate([chosen, padding], axis=0).T
        for k in range(GROUP):
            limits[i, pl.ds(k * rows, rows), :] = turned[part(member ^ k, rows), :]


def fetch(heads, rows, count, keys_copy, values_copy, key_bounds, value_bounds):
    width = keys_copy.shape[2]
    return pl.pallas_call(
        functools.partial(fetch_kernel, heads, count),
        out_shape=[
            jax.ShapeDtypeStruct((1 + count, GROUP * rows, width), keys_copy.dtype),
            jax.ShapeDtypeStruct((1 + count, GROUP * rows, 128), key_bounds.dtype),
        ],
        in_specs=[HBM] * 4,
        out_specs=[VMEM] * 2,
        scratch_shapes=[
            pltpu.VMEM((1 + count, key_bounds.shape[1], GROUP * rows), key_bounds.dtype),
            pltpu.VMEM((GROUP * rows, 128), key_bounds.dtype),
            pltpu.SemaphoreType.DMA(((1 + GROUP) * (1 + count),)),
        ],
        compiler_params=limit(4 * MB + MB * count),
        cost_estimate=cost(1000),
        name="fetch",
    )(keys_copy, values_copy, key_bounds.T, value_bounds.T)


def restore(heads, pieces, old, limits, out, start):
    rows, width = pieces[0].shape
    head = width // heads
    for k, piece in enumerate(pieces):
        place = slice(k * rows, (k + 1) * rows)
        for h in range(heads):
            lanes = slice(h * head, (h + 1) * head)
            bound = limits[place, h : h + 1]
            previous = old[place, lanes].astype(jnp.float32)
            change = jnp.clip(piece[:, lanes].astype(jnp.float32) - previous, -bound, bound)
            change = change.astype(jnp.bfloat16).astype(jnp.float32)
            out[start + k * rows : start + (k + 1) * rows, lanes] = (previous + change).astype(out.dtype)


def rebuild_keys_kernel(heads, kept, beside, opposite, old, limits, _, out):
    rows = kept.shape[2]
    pieces = [kept.at[0, 0], beside.at[0, 0], opposite.at[pl.ds(0, rows)], opposite.at[pl.ds(rows, rows)]]
    restore(heads, pieces, old.at[0], limits.at[0], out, 0)


def rebuild_values_kernel(heads, first, this, opposite, old, limits, *refs):
    out = refs[-1]
    rows = old.shape[1] // GROUP
    for j in range(this.shape[1] // (2 * rows)):
        starts = [2 * j * rows, (2 * j + 1) * rows]
        pieces = [this.at[0, pl.ds(start, rows)] for start in starts]
        pieces += [opposite.at[pl.ds(start, rows)] for start in starts]
        restore(heads, pieces, old.at[1 + first + j], limits.at[1 + first + j], out, j * GROUP * rows)


def rebuild(kernel, tokens, old, *operands):
    return pl.pallas_call(
        kernel,
        out_shape=jax.ShapeDtypeStruct((tokens, old.shape[2]), old.dtype),
        in_specs=[VMEM] * len(operands),
        out_specs=VMEM,
        compiler_params=limit(4 * MB + 16 * tokens * old.shape[2]),
        cost_estimate=cost(1000),
        name="rebuild",
    )(*operands)


def attend_kernel(heads, parts, query_ref, near_keys, near_values, far_keys, far_values, *refs):
    refs = refs[-len(parts) :]
    width = near_keys.shape[1]
    rows = query_ref.shape[0] // GROUP
    head = width // heads
    outs = {k: ref.at[j] for ref, group in zip(refs, parts) for j, k in enumerate(group)}
    scale = head ** (-0.5) * LOG2E
    lane = lax.broadcasted_iota(jnp.int32, (GROUP * rows, head), 1)
    stats = jnp.zeros((GROUP * rows, head), jnp.float32)
    contract = (((1,), (1,)), ((), ()))
    for h in range(heads):
        lanes = slice(h * head, (h + 1) * head)
        query = query_ref[:, lanes]
        keys = jnp.concatenate([near_keys[:, lanes], far_keys[:, lanes]], axis=0)
        values = jnp.concatenate([near_values[:, lanes], far_values[:, lanes]], axis=0)
        score = lax.dot_general(query, keys, contract, preferred_element_type=jnp.float32)
        peak = jnp.max(score, axis=1, keepdims=True)
        level = (peak * scale).astype(jnp.bfloat16).astype(jnp.float32)
        probs = jnp.exp2(score * scale - level).astype(jnp.bfloat16)
        joined = jnp.concatenate([values, jnp.ones_like(values)], axis=1)
        total = jnp.dot(probs, joined, preferred_element_type=jnp.float32)
        weighted = total[:, :head].astype(jnp.bfloat16)
        weight = total[:, head:]
        high = weight.astype(jnp.bfloat16).astype(jnp.float32)
        stats = jnp.where(lane == h, level, stats)
        stats = jnp.where(lane == heads + h, high, stats)
        stats = jnp.where(lane == 2 * heads + h, weight - high, stats)
        for k, out in sorted(outs.items()):
            out[h * rows : (h + 1) * rows, :] = weighted[k * rows : (k + 1) * rows]
    half = rows // 2
    for k, out in sorted(outs.items()):
        first = stats[k * rows : k * rows + half]
        second = stats[k * rows + half : (k + 1) * rows]
        packed = first + pltpu.roll(second, 16, 1)
        out[heads * rows :, :] = packed.astype(out.dtype)


def attend(heads, parts, query, near, far, *earlier):
    tokens, width = near[0].shape
    rows = query.shape[0] // GROUP
    shape = (heads * rows + rows // 2, width // heads)
    outs = [jax.ShapeDtypeStruct((len(group),) + shape, near[0].dtype) for group in parts]
    room = 4 * MB + 32 * tokens * width + 64 * GROUP * rows * tokens
    return pl.pallas_call(
        functools.partial(attend_kernel, heads, parts),
        out_shape=outs,
        in_specs=[VMEM] * 5 + [HBM] * len(earlier),
        out_specs=[VMEM] * len(outs),
        compiler_params=limit(room),
        cost_estimate=cost(1000),
        name="attend",
    )(query, *near, *far, *earlier)


def merge_kernel(heads, n0, n1, n2, n3, f0, f1, f2, f3, out):
    rows = out.shape[0]
    head = n0.shape[2]
    width = heads * head
    _, member = position()

    def unpack(ref):
        packed = ref[0, heads * rows :, :].astype(jnp.float32)
        stats = jnp.concatenate([packed, pltpu.roll(packed, head - 16, 1)], axis=0)
        weight = pltpu.roll(stats, head - heads, 1) + pltpu.roll(stats, head - 2 * heads, 1)
        return stats, weight

    for k, (near, far) in enumerate(((n0, f0), (n1, f1), (n2, f2), (n3, f3))):
        near_level, near_weight = unpack(near)
        far_level, far_weight = unpack(far)
        top = jnp.maximum(near_level, far_level)
        near_scale = jnp.exp2(near_level - top)
        far_scale = jnp.exp2(far_level - top)
        total = near_scale * near_weight + far_scale * far_weight
        near_scale = near_scale / total
        far_scale = far_scale / total
        for h in range(heads):
            place = slice(h * rows, (h + 1) * rows)
            mixed = near[0, place, :].astype(jnp.float32) * near_scale[:, h : h + 1]
            mixed = mixed + far[0, place, :].astype(jnp.float32) * far_scale[:, h : h + 1]
            start = pl.multiple_of((member ^ k) * width + h * head, head)
            out[:, pl.ds(start, head)] = mixed.astype(out.dtype)


def merge(heads, near, far, rows):
    head = near[0].shape[2]
    return pl.pallas_call(
        functools.partial(merge_kernel, heads),
        out_shape=jax.ShapeDtypeStruct((rows, GROUP * heads * head), near[0].dtype),
        in_specs=[VMEM] * 8,
        out_specs=VMEM,
        compiler_params=limit(4 * MB),
        cost_estimate=cost(1000),
        name="merge",
    )(*near, *far)


def shards(queries, keys_new, values_new, keys_copy, values_copy, key_bounds, value_bounds):
    rows = queries.shape[0]
    heads = key_bounds.shape[1] // GROUP
    levels = lax.axis_size("patch").bit_length() - 1
    across = 1 << levels - 1

    pinned = [pltpu.with_memory_space_constraint(a, pltpu.HBM) for a in (keys_new, values_new, queries)]
    copies = [pltpu.with_memory_space_constraint(a, pltpu.HBM) for a in (keys_copy, values_copy)]
    sent, kept = cut(*pinned)
    beside = swapped(sent, 1)
    x_query, x_keys, x_own, near_raw = join(kept, beside)
    own_query = assemble(kept, beside, swapped(x_query, 2))
    far_query = swapped(own_query, across)
    bits = [1 << bit for bit in range(2, levels - 1)]
    for bit in bits[:-1]:
        near_raw = jnp.concatenate([near_raw, swapped(near_raw, bit)], axis=1)
    far_raw = swapped(near_raw, bits[-1])
    if len(bits) > 1:
        x_own = near_raw[1]
    x_keys, x_own = swapped(x_keys, 2), swapped(x_own, 2)
    count = 1 << len(bits)
    old, limits = fetch(heads, rows, count, *copies, key_bounds, value_bounds)
    block = GROUP * rows
    rebuild_keys = functools.partial(rebuild_keys_kernel, heads)
    near_keys = rebuild(rebuild_keys, block, old, kept, beside, x_keys, old, limits, own_query)
    picked = pick(far_raw, near_keys)
    for bit in bits[:-1]:
        near_keys = jnp.concatenate([near_keys, swapped(near_keys, bit)], axis=0)
    far_keys = swapped(near_keys, bits[-1])
    halves = []
    sides = ((0, near_raw, x_own, own_query), (count // 2, far_raw, swapped(picked, 2), far_query))
    for first, this, opposite, earlier in sides:
        kernel = functools.partial(rebuild_values_kernel, heads, first)
        halves.append(rebuild(kernel, block * count // 2, old, this, opposite, old, limits, earlier))
    near, far = (near_keys, halves[0]), (far_keys, halves[1])
    parts = ((2, 3), (0,), (1,))
    far_out = attend(heads, parts, far_query, near, far)
    f23, f0, f1 = [swapped(a, across + group[0]) for a, group in zip(far_out, parts)]
    parts = ((0,), (1,), (2, 3))
    n0, n1, n23 = attend(heads, parts, own_query, near, far, far_out[2])
    n1, n23 = swapped(n1, 1), swapped(n23, 2)
    f3 = pick(f23)
    n3 = pick(n23, f3)
    near_parts = (n0, n1, n23, swapped(n3, 1)[None])
    far_parts = (f0, f1, f23, swapped(f3, 1)[None])
    return merge(heads, near_parts, far_parts, rows)


def solution(mesh):
    rows = P(("clips", "patch"), None)
    copies = P(("clips", "patch"), None, None)
    bounds = P("clips", None)
    return jax.shard_map(
        shards,
        mesh=mesh,
        in_specs=(rows, rows, rows, copies, copies, bounds, bounds),
        out_specs=rows,
        check_vma=False,
    )
```

```python
import functools

import jax
import jax.numpy as jnp
from jax import lax
from jax.experimental import pallas as pl
from jax.experimental.pallas import tpu as pltpu
from jax.sharding import PartitionSpec as P

GROUP = 4
LOG2E = 1.4426950408889634
MB = 1 << 20
HBM = pl.BlockSpec(memory_space=pltpu.HBM)
VMEM = pl.BlockSpec(memory_space=pltpu.VMEM)


def limit(size):
    return pltpu.CompilerParams(vmem_limit_bytes=size)


def cost(size):
    return pl.CostEstimate(flops=0, bytes_accessed=size, transcendentals=0)


def swapped(array, mask):
    size = lax.axis_size("patch")
    return lax.ppermute(array, "patch", [(i, i ^ mask) for i in range(size)])


def position():
    place = lax.axis_index("patch")
    return place // GROUP, place % GROUP


def part(index, size):
    return pl.ds(pl.multiple_of(index * size, size), size)


def run_copies(pairs, sems):
    copies = [pltpu.make_async_copy(a, b, sems.at[i]) for i, (a, b) in enumerate(pairs)]
    for copy in copies:
        copy.start()
    for copy in copies:
        copy.wait()


def cut_kernel(count, *refs):
    slabs, sent, kept, sems = refs[:count], refs[-3], refs[-2], refs[-1]
    width = slabs[0].shape[1] // GROUP
    _, member = position()
    pairs = []
    for i, slab in enumerate(slabs):
        for k in range(2):
            pairs.append((slab.at[:, part(member ^ (1 + 2 * k), width)], sent.at[i, k]))
            pairs.append((slab.at[:, part(member ^ (2 * k), width)], kept.at[i, k]))
    run_copies(pairs, sems)


def cut(*slabs):
    rows, features = slabs[0].shape
    shape = jax.ShapeDtypeStruct((len(slabs), 2, rows, features // GROUP), slabs[0].dtype)
    return pl.pallas_call(
        functools.partial(cut_kernel, len(slabs)),
        out_shape=[shape] * 2,
        in_specs=[HBM] * len(slabs),
        out_specs=[VMEM] * 2,
        scratch_shapes=[pltpu.SemaphoreType.DMA((4 * len(slabs),))],
        compiler_params=limit(4 * MB),
        cost_estimate=cost(1000),
        name="cut",
    )(*slabs)


def join_kernel(kept, arrived, x_query, x_keys, x_values, z_values):
    rows = kept.shape[2]
    for i, out in ((0, x_keys), (1, x_values), (2, x_query)):
        out[:rows] = kept[i, 1]
        out[rows:] = arrived[i, 1]
    for k in range(2):
        z_values[k, :rows] = kept[1, k]
        z_values[k, rows:] = arrived[1, k]


def join(kept, arrived):
    _, _, rows, width = kept.shape
    shape = (2 * rows, width)
    return pl.pallas_call(
        join_kernel,
        out_shape=[jax.ShapeDtypeStruct(shape, kept.dtype)] * 3 + [jax.ShapeDtypeStruct((2,) + shape, kept.dtype)],
        in_specs=[VMEM] * 2,
        out_specs=[VMEM] * 4,
        compiler_params=limit(4 * MB),
        cost_estimate=cost(1000),
        name="join",
    )(kept, arrived)


def assemble_kernel(kept, beside, opposite, out):
    rows = kept.shape[2]
    out[:rows] = kept[2, 0]
    out[rows : 2 * rows] = beside[2, 0]
    out[2 * rows :] = opposite[...]


def assemble(kept, beside, opposite):
    _, _, rows, width = kept.shape
    return pl.pallas_call(
        assemble_kernel,
        out_shape=jax.ShapeDtypeStruct((GROUP * rows, width), kept.dtype),
        in_specs=[VMEM] * 3,
        out_specs=VMEM,
        compiler_params=limit(4 * MB),
        cost_estimate=cost(1000),
        name="assemble",
    )(kept, beside, opposite)


def pick_kernel(both, *refs):
    refs[-1][...] = both[1]


def pick(both, *earlier):
    return pl.pallas_call(
        pick_kernel,
        out_shape=jax.ShapeDtypeStruct(both.shape[1:], both.dtype),
        in_specs=[VMEM] + [HBM] * len(earlier),
        out_specs=VMEM,
        compiler_params=limit(4 * MB + 2 * both.size * both.dtype.itemsize),
        cost_estimate=cost(4_000_000),
        name="pick",
    )(both, *earlier)


def fetch_kernel(heads, count, keys_copy, values_copy, kb, vb, old, limits, lines, turned, sems):
    rows = old.shape[1] // GROUP
    group, member = position()
    sources = [(keys_copy, kb, group)] + [(values_copy, vb, group ^ j) for j in range(count)]
    pairs = []
    for i, (copy, bound, block) in enumerate(sources):
        pairs.append((bound.at[:, part(block, GROUP * rows)], lines.at[i]))
        for k in range(GROUP):
            source = copy.at[0, part(block * GROUP + (member ^ k), rows), :]
            pairs.append((source, old.at[i, pl.ds(k * rows, rows), :]))
    run_copies(pairs, sems)
    for i in range(len(sources)):
        chosen = lines[i, pl.ds(member * heads, heads), :]
        padding = jnp.zeros((limits.shape[2] - heads, GROUP * rows), chosen.dtype)
        turned[...] = jnp.concatenate([chosen, padding], axis=0).T
        for k in range(GROUP):
            limits[i, pl.ds(k * rows, rows), :] = turned[part(member ^ k, rows), :]


def fetch(heads, rows, count, keys_copy, values_copy, key_bounds, value_bounds):
    width = keys_copy.shape[2]
    return pl.pallas_call(
        functools.partial(fetch_kernel, heads, count),
        out_shape=[
            jax.ShapeDtypeStruct((1 + count, GROUP * rows, width), keys_copy.dtype),
            jax.ShapeDtypeStruct((1 + count, GROUP * rows, 128), key_bounds.dtype),
        ],
        in_specs=[HBM] * 4,
        out_specs=[VMEM] * 2,
        scratch_shapes=[
            pltpu.VMEM((1 + count, key_bounds.shape[1], GROUP * rows), key_bounds.dtype),
            pltpu.VMEM((GROUP * rows, 128), key_bounds.dtype),
            pltpu.SemaphoreType.DMA(((1 + GROUP) * (1 + count),)),
        ],
        compiler_params=limit(4 * MB + MB * count),
        cost_estimate=cost(1000),
        name="fetch",
    )(keys_copy, values_copy, key_bounds.T, value_bounds.T)


def restore(heads, pieces, old, limits, out, start):
    rows, width = pieces[0].shape
    head = width // heads
    for k, piece in enumerate(pieces):
        place = slice(k * rows, (k + 1) * rows)
        for h in range(heads):
            lanes = slice(h * head, (h + 1) * head)
            bound = limits[place, h : h + 1]
            previous = old[place, lanes].astype(jnp.float32)
            change = jnp.clip(piece[:, lanes].astype(jnp.float32) - previous, -bound, bound)
            change = change.astype(jnp.bfloat16).astype(jnp.float32)
            out[start + k * rows : start + (k + 1) * rows, lanes] = (previous + change).astype(out.dtype)


def rebuild_keys_kernel(heads, kept, beside, opposite, old, limits, _, out):
    rows = kept.shape[2]
    pieces = [kept.at[0, 0], beside.at[0, 0], opposite.at[pl.ds(0, rows)], opposite.at[pl.ds(rows, rows)]]
    restore(heads, pieces, old.at[0], limits.at[0], out, 0)


def rebuild_values_kernel(heads, first, this, opposite, old, limits, *refs):
    out = refs[-1]
    rows = old.shape[1] // GROUP
    for j in range(this.shape[1] // (2 * rows)):
        starts = [2 * j * rows, (2 * j + 1) * rows]
        pieces = [this.at[0, pl.ds(start, rows)] for start in starts]
        pieces += [opposite.at[pl.ds(start, rows)] for start in starts]
        restore(heads, pieces, old.at[1 + first + j], limits.at[1 + first + j], out, j * GROUP * rows)


def rebuild(kernel, tokens, old, *operands):
    return pl.pallas_call(
        kernel,
        out_shape=jax.ShapeDtypeStruct((tokens, old.shape[2]), old.dtype),
        in_specs=[VMEM] * len(operands),
        out_specs=VMEM,
        compiler_params=limit(4 * MB + 16 * tokens * old.shape[2]),
        cost_estimate=cost(1000),
        name="rebuild",
    )(*operands)


def attend_kernel(heads, parts, query_ref, near_keys, near_values, far_keys, far_values, *refs):
    refs = refs[-len(parts) :]
    width = near_keys.shape[1]
    rows = query_ref.shape[0] // GROUP
    head = width // heads
    outs = {k: ref.at[j] for ref, group in zip(refs, parts) for j, k in enumerate(group)}
    scale = head ** (-0.5) * LOG2E
    lane = lax.broadcasted_iota(jnp.int32, (GROUP * rows, head), 1)
    stats = jnp.zeros((GROUP * rows, head), jnp.float32)
    contract = (((1,), (1,)), ((), ()))
    def stacked(near, far, h):
        lanes = slice(h * head, (h + 1) * head)
        return jnp.concatenate([near[:, lanes], far[:, lanes]], axis=0)

    scores = []
    for h in range(heads):
        query = query_ref[:, h * head : (h + 1) * head]
        keys = stacked(near_keys, far_keys, h)
        scores.append(lax.dot_general(query, keys, contract, preferred_element_type=jnp.float32))
    peaks = [jnp.max(score, axis=1, keepdims=True) for score in scores]
    levels = [(peak * scale).astype(jnp.bfloat16).astype(jnp.float32) for peak in peaks]
    probs = [jnp.exp2(score * scale - level).astype(jnp.bfloat16) for score, level in zip(scores, levels)]
    totals = []
    for h in range(heads):
        values = stacked(near_values, far_values, h)
        joined = jnp.concatenate([values, jnp.ones_like(values)], axis=1)
        totals.append(jnp.dot(probs[h], joined, preferred_element_type=jnp.float32))
    for h in range(heads):
        weight = totals[h][:, head:]
        high = weight.astype(jnp.bfloat16).astype(jnp.float32)
        stats = jnp.where(lane == h, levels[h], stats)
        stats = jnp.where(lane == heads + h, high, stats)
        stats = jnp.where(lane == 2 * heads + h, weight - high, stats)
    for h in range(heads):
        weighted = totals[h][:, :head].astype(jnp.bfloat16)
        for k, out in sorted(outs.items()):
            out[h * rows : (h + 1) * rows, :] = weighted[k * rows : (k + 1) * rows]
    half = rows // 2
    for k, out in sorted(outs.items()):
        first = stats[k * rows : k * rows + half]
        second = stats[k * rows + half : (k + 1) * rows]
        packed = first + pltpu.roll(second, 16, 1)
        out[heads * rows :, :] = packed.astype(out.dtype)


def attend(heads, parts, query, near, far, *earlier):
    tokens, width = near[0].shape
    rows = query.shape[0] // GROUP
    shape = (heads * rows + rows // 2, width // heads)
    outs = [jax.ShapeDtypeStruct((len(group),) + shape, near[0].dtype) for group in parts]
    room = 4 * MB + 32 * tokens * width + 64 * GROUP * rows * tokens
    return pl.pallas_call(
        functools.partial(attend_kernel, heads, parts),
        out_shape=outs,
        in_specs=[VMEM] * 5 + [HBM] * len(earlier),
        out_specs=[VMEM] * len(outs),
        compiler_params=limit(room),
        cost_estimate=cost(1000),
        name="attend",
    )(query, *near, *far, *earlier)


def merge_kernel(heads, n0, n1, n2, n3, f0, f1, f2, f3, out):
    rows = out.shape[0]
    head = n0.shape[2]
    width = heads * head
    _, member = position()

    def unpack(ref):
        packed = ref[0, heads * rows :, :].astype(jnp.float32)
        stats = jnp.concatenate([packed, pltpu.roll(packed, head - 16, 1)], axis=0)
        weight = pltpu.roll(stats, head - heads, 1) + pltpu.roll(stats, head - 2 * heads, 1)
        return stats, weight

    mixtures = []
    for k, (near, far) in enumerate(((n0, f0), (n1, f1), (n2, f2), (n3, f3))):
        near_level, near_weight = unpack(near)
        far_level, far_weight = unpack(far)
        top = jnp.maximum(near_level, far_level)
        near_scale = jnp.exp2(near_level - top)
        far_scale = jnp.exp2(far_level - top)
        total = near_scale * near_weight + far_scale * far_weight
        near_scale = near_scale / total
        far_scale = far_scale / total
        for h in range(heads):
            place = slice(h * rows, (h + 1) * rows)
            mixed = near[0, place, :].astype(jnp.float32) * near_scale[:, h : h + 1]
            mixed = mixed + far[0, place, :].astype(jnp.float32) * far_scale[:, h : h + 1]
            mixtures.append((k, h, mixed.astype(out.dtype)))
    for k, h, mixed in mixtures:
        start = pl.multiple_of((member ^ k) * width + h * head, head)
        out[:, pl.ds(start, head)] = mixed


def merge(heads, near, far, rows):
    head = near[0].shape[2]
    return pl.pallas_call(
        functools.partial(merge_kernel, heads),
        out_shape=jax.ShapeDtypeStruct((rows, GROUP * heads * head), near[0].dtype),
        in_specs=[VMEM] * 8,
        out_specs=VMEM,
        compiler_params=limit(4 * MB),
        cost_estimate=cost(1000),
        name="merge",
    )(*near, *far)


def shards(queries, keys_new, values_new, keys_copy, values_copy, key_bounds, value_bounds):
    rows = queries.shape[0]
    heads = key_bounds.shape[1] // GROUP
    levels = lax.axis_size("patch").bit_length() - 1
    across = 1 << levels - 1

    pinned = [pltpu.with_memory_space_constraint(a, pltpu.HBM) for a in (keys_new, values_new, queries)]
    copies = [pltpu.with_memory_space_constraint(a, pltpu.HBM) for a in (keys_copy, values_copy)]
    sent, kept = cut(*pinned)
    beside = swapped(sent, 1)
    x_query, x_keys, x_own, near_raw = join(kept, beside)
    own_query = assemble(kept, beside, swapped(x_query, 2))
    far_query = swapped(own_query, across)
    bits = [1 << bit for bit in range(2, levels - 1)]
    for bit in bits[:-1]:
        near_raw = jnp.concatenate([near_raw, swapped(near_raw, bit)], axis=1)
    far_raw = swapped(near_raw, bits[-1])
    if len(bits) > 1:
        x_own = near_raw[1]
    x_keys, x_own = swapped(x_keys, 2), swapped(x_own, 2)
    count = 1 << len(bits)
    old, limits = fetch(heads, rows, count, *copies, key_bounds, value_bounds)
    block = GROUP * rows
    rebuild_keys = functools.partial(rebuild_keys_kernel, heads)
    near_keys = rebuild(rebuild_keys, block, old, kept, beside, x_keys, old, limits, own_query)
    picked = pick(far_raw, near_keys)
    for bit in bits[:-1]:
        near_keys = jnp.concatenate([near_keys, swapped(near_keys, bit)], axis=0)
    far_keys = swapped(near_keys, bits[-1])
    halves = []
    sides = ((0, near_raw, x_own, own_query), (count // 2, far_raw, swapped(picked, 2), far_query))
    for first, this, opposite, earlier in sides:
        kernel = functools.partial(rebuild_values_kernel, heads, first)
        halves.append(rebuild(kernel, block * count // 2, old, this, opposite, old, limits, earlier))
    near, far = (near_keys, halves[0]), (far_keys, halves[1])
    parts = ((2, 3), (0,), (1,))
    far_out = attend(heads, parts, far_query, near, far)
    f23, f0, f1 = [swapped(a, across + group[0]) for a, group in zip(far_out, parts)]
    parts = ((0,), (1,), (2, 3))
    n0, n1, n23 = attend(heads, parts, own_query, near, far, far_out[2])
    n1, n23 = swapped(n1, 1), swapped(n23, 2)
    f3 = pick(f23)
    n3 = pick(n23, f3)
    near_parts = (n0, n1, n23, swapped(n3, 1)[None])
    far_parts = (f0, f1, f23, swapped(f3, 1)[None])
    return merge(heads, near_parts, far_parts, rows)


def solution(mesh):
    rows = P(("clips", "patch"), None)
    copies = P(("clips", "patch"), None, None)
    bounds = P("clips", None)
    return jax.shard_map(
        shards,
        mesh=mesh,
        in_specs=(rows, rows, rows, copies, copies, bounds, bounds),
        out_specs=rows,
        check_vma=False,
    )
```

```python
import functools

import jax
import jax.numpy as jnp
from jax import lax
from jax.experimental import pallas as pl
from jax.experimental.pallas import tpu as pltpu
from jax.sharding import PartitionSpec as P

GROUP = 4
LOG2E = 1.4426950408889634
MB = 1 << 20
HBM = pl.BlockSpec(memory_space=pltpu.HBM)
VMEM = pl.BlockSpec(memory_space=pltpu.VMEM)


def limit(size):
    return pltpu.CompilerParams(vmem_limit_bytes=size)


def cost(size):
    return pl.CostEstimate(flops=0, bytes_accessed=size, transcendentals=0)


def swapped(array, mask):
    size = lax.axis_size("patch")
    return lax.ppermute(array, "patch", [(i, i ^ mask) for i in range(size)])


def position():
    place = lax.axis_index("patch")
    return place // GROUP, place % GROUP


def part(index, size):
    return pl.ds(pl.multiple_of(index * size, size), size)


def run_copies(pairs, sems):
    copies = [pltpu.make_async_copy(a, b, sems.at[i]) for i, (a, b) in enumerate(pairs)]
    for copy in copies:
        copy.start()
    for copy in copies:
        copy.wait()


def cut_kernel(count, first, *refs):
    slabs, out, sems = refs[:count], refs[-2], refs[-1]
    width = slabs[0].shape[1] // GROUP
    _, member = position()
    pairs = []
    for i, slab in enumerate(slabs):
        for k in range(2):
            pairs.append((slab.at[:, part(member ^ (first + 2 * k), width)], out.at[i, k]))
    run_copies(pairs, sems)


def cut(first, slabs, *earlier):
    rows, features = slabs[0].shape
    shape = jax.ShapeDtypeStruct((len(slabs), 2, rows, features // GROUP), slabs[0].dtype)
    return pl.pallas_call(
        functools.partial(cut_kernel, len(slabs), first),
        out_shape=shape,
        in_specs=[HBM] * (len(slabs) + len(earlier)),
        out_specs=VMEM,
        scratch_shapes=[pltpu.SemaphoreType.DMA((2 * len(slabs),))],
        compiler_params=limit(4 * MB),
        cost_estimate=cost(1000),
        name="cut",
    )(*slabs, *earlier)


def join_kernel(kept, arrived, x_query, x_keys, x_values, z_values):
    rows = kept.shape[2]
    for i, out in ((0, x_keys), (1, x_values), (2, x_query)):
        out[:rows] = kept[i, 1]
        out[rows:] = arrived[i, 1]
    for k in range(2):
        z_values[k, :rows] = kept[1, k]
        z_values[k, rows:] = arrived[1, k]


def join(kept, arrived):
    _, _, rows, width = kept.shape
    shape = (2 * rows, width)
    return pl.pallas_call(
        join_kernel,
        out_shape=[jax.ShapeDtypeStruct(shape, kept.dtype)] * 3 + [jax.ShapeDtypeStruct((2,) + shape, kept.dtype)],
        in_specs=[VMEM] * 2,
        out_specs=[VMEM] * 4,
        compiler_params=limit(4 * MB),
        cost_estimate=cost(1000),
        name="join",
    )(kept, arrived)


def assemble_kernel(kept, beside, opposite, out):
    rows = kept.shape[2]
    out[:rows] = kept[2, 0]
    out[rows : 2 * rows] = beside[2, 0]
    out[2 * rows :] = opposite[...]


def assemble(kept, beside, opposite):
    _, _, rows, width = kept.shape
    return pl.pallas_call(
        assemble_kernel,
        out_shape=jax.ShapeDtypeStruct((GROUP * rows, width), kept.dtype),
        in_specs=[VMEM] * 3,
        out_specs=VMEM,
        compiler_params=limit(4 * MB),
        cost_estimate=cost(1000),
        name="assemble",
    )(kept, beside, opposite)


def pick_kernel(both, *refs):
    refs[-1][...] = both[1]


def pick(both, *earlier):
    return pl.pallas_call(
        pick_kernel,
        out_shape=jax.ShapeDtypeStruct(both.shape[1:], both.dtype),
        in_specs=[VMEM] + [HBM] * len(earlier),
        out_specs=VMEM,
        compiler_params=limit(4 * MB + 2 * both.size * both.dtype.itemsize),
        cost_estimate=cost(4_000_000),
        name="pick",
    )(both, *earlier)


def fetch_kernel(heads, count, keys_copy, values_copy, kb, vb, old, limits, lines, turned, sems):
    rows = old.shape[1] // GROUP
    group, member = position()
    sources = [(keys_copy, kb, group)] + [(values_copy, vb, group ^ j) for j in range(count)]
    pairs = []
    for i, (copy, bound, block) in enumerate(sources):
        pairs.append((bound.at[:, part(block, GROUP * rows)], lines.at[i]))
        for k in range(GROUP):
            source = copy.at[0, part(block * GROUP + (member ^ k), rows), :]
            pairs.append((source, old.at[i, pl.ds(k * rows, rows), :]))
    run_copies(pairs, sems)
    for i in range(len(sources)):
        chosen = lines[i, pl.ds(member * heads, heads), :]
        padding = jnp.zeros((limits.shape[2] - heads, GROUP * rows), chosen.dtype)
        turned[...] = jnp.concatenate([chosen, padding], axis=0).T
        for k in range(GROUP):
            limits[i, pl.ds(k * rows, rows), :] = turned[part(member ^ k, rows), :]


def fetch(heads, rows, count, keys_copy, values_copy, key_bounds, value_bounds):
    width = keys_copy.shape[2]
    return pl.pallas_call(
        functools.partial(fetch_kernel, heads, count),
        out_shape=[
            jax.ShapeDtypeStruct((1 + count, GROUP * rows, width), keys_copy.dtype),
            jax.ShapeDtypeStruct((1 + count, GROUP * rows, 128), key_bounds.dtype),
        ],
        in_specs=[HBM] * 4,
        out_specs=[VMEM] * 2,
        scratch_shapes=[
            pltpu.VMEM((1 + count, key_bounds.shape[1], GROUP * rows), key_bounds.dtype),
            pltpu.VMEM((GROUP * rows, 128), key_bounds.dtype),
            pltpu.SemaphoreType.DMA(((1 + GROUP) * (1 + count),)),
        ],
        compiler_params=limit(4 * MB + MB * count),
        cost_estimate=cost(1000),
        name="fetch",
    )(keys_copy, values_copy, key_bounds.T, value_bounds.T)


def restore(heads, pieces, old, limits, out, start):
    rows, width = pieces[0].shape
    head = width // heads
    for k, piece in enumerate(pieces):
        place = slice(k * rows, (k + 1) * rows)
        for h in range(heads):
            lanes = slice(h * head, (h + 1) * head)
            bound = limits[place, h : h + 1]
            previous = old[place, lanes].astype(jnp.float32)
            change = jnp.clip(piece[:, lanes].astype(jnp.float32) - previous, -bound, bound)
            change = change.astype(jnp.bfloat16).astype(jnp.float32)
            out[start + k * rows : start + (k + 1) * rows, lanes] = (previous + change).astype(out.dtype)


def rebuild_keys_kernel(heads, kept, beside, opposite, old, limits, _, out):
    rows = kept.shape[2]
    pieces = [kept.at[0, 0], beside.at[0, 0], opposite.at[pl.ds(0, rows)], opposite.at[pl.ds(rows, rows)]]
    restore(heads, pieces, old.at[0], limits.at[0], out, 0)


def rebuild_values_kernel(heads, first, this, opposite, old, limits, *refs):
    out = refs[-1]
    rows = old.shape[1] // GROUP
    for j in range(this.shape[1] // (2 * rows)):
        starts = [2 * j * rows, (2 * j + 1) * rows]
        pieces = [this.at[0, pl.ds(start, rows)] for start in starts]
        pieces += [opposite.at[pl.ds(start, rows)] for start in starts]
        restore(heads, pieces, old.at[1 + first + j], limits.at[1 + first + j], out, j * GROUP * rows)


def rebuild(kernel, tokens, old, *operands):
    return pl.pallas_call(
        kernel,
        out_shape=jax.ShapeDtypeStruct((tokens, old.shape[2]), old.dtype),
        in_specs=[VMEM] * len(operands),
        out_specs=VMEM,
        compiler_params=limit(4 * MB + 16 * tokens * old.shape[2]),
        cost_estimate=cost(1000),
        name="rebuild",
    )(*operands)


def attend_kernel(heads, parts, query_ref, near_keys, near_values, far_keys, far_values, *refs):
    refs = refs[-len(parts) :]
    width = near_keys.shape[1]
    rows = query_ref.shape[0] // GROUP
    head = width // heads
    outs = {k: ref.at[j] for ref, group in zip(refs, parts) for j, k in enumerate(group)}
    scale = head ** (-0.5) * LOG2E
    lane = lax.broadcasted_iota(jnp.int32, (GROUP * rows, head), 1)
    stats = jnp.zeros((GROUP * rows, head), jnp.float32)
    contract = (((1,), (1,)), ((), ()))
    def stacked(near, far, h):
        lanes = slice(h * head, (h + 1) * head)
        return jnp.concatenate([near[:, lanes], far[:, lanes]], axis=0)

    scores = []
    for h in range(heads):
        query = query_ref[:, h * head : (h + 1) * head]
        keys = stacked(near_keys, far_keys, h)
        scores.append(lax.dot_general(query, keys, contract, preferred_element_type=jnp.float32))
    peaks = [jnp.max(score, axis=1, keepdims=True) for score in scores]
    levels = [(peak * scale).astype(jnp.bfloat16).astype(jnp.float32) for peak in peaks]
    probs = [jnp.exp2(score * scale - level).astype(jnp.bfloat16) for score, level in zip(scores, levels)]
    totals = []
    for h in range(heads):
        values = stacked(near_values, far_values, h)
        joined = jnp.concatenate([values, jnp.ones_like(values)], axis=1)
        totals.append(jnp.dot(probs[h], joined, preferred_element_type=jnp.float32))
    for h in range(heads):
        weight = totals[h][:, head:]
        high = weight.astype(jnp.bfloat16).astype(jnp.float32)
        stats = jnp.where(lane == h, levels[h], stats)
        stats = jnp.where(lane == heads + h, high, stats)
        stats = jnp.where(lane == 2 * heads + h, weight - high, stats)
    for h in range(heads):
        weighted = totals[h][:, :head].astype(jnp.bfloat16)
        for k, out in sorted(outs.items()):
            out[h * rows : (h + 1) * rows, :] = weighted[k * rows : (k + 1) * rows]
    half = rows // 2
    for k, out in sorted(outs.items()):
        first = stats[k * rows : k * rows + half]
        second = stats[k * rows + half : (k + 1) * rows]
        packed = first + pltpu.roll(second, 16, 1)
        out[heads * rows :, :] = packed.astype(out.dtype)


def attend(heads, parts, query, near, far, *earlier):
    tokens, width = near[0].shape
    rows = query.shape[0] // GROUP
    shape = (heads * rows + rows // 2, width // heads)
    outs = [jax.ShapeDtypeStruct((len(group),) + shape, near[0].dtype) for group in parts]
    room = 4 * MB + 32 * tokens * width + 64 * GROUP * rows * tokens
    return pl.pallas_call(
        functools.partial(attend_kernel, heads, parts),
        out_shape=outs,
        in_specs=[VMEM] * 5 + [HBM] * len(earlier),
        out_specs=[VMEM] * len(outs),
        compiler_params=limit(room),
        cost_estimate=cost(1000),
        name="attend",
    )(query, *near, *far, *earlier)


def merge_kernel(heads, n0, n1, n2, n3, f0, f1, f2, f3, out):
    rows = out.shape[0]
    head = n0.shape[2]
    width = heads * head
    _, member = position()

    def unpack(ref):
        packed = ref[0, heads * rows :, :].astype(jnp.float32)
        stats = jnp.concatenate([packed, pltpu.roll(packed, head - 16, 1)], axis=0)
        weight = pltpu.roll(stats, head - heads, 1) + pltpu.roll(stats, head - 2 * heads, 1)
        return stats, weight

    mixtures = []
    for k, (near, far) in enumerate(((n0, f0), (n1, f1), (n2, f2), (n3, f3))):
        near_level, near_weight = unpack(near)
        far_level, far_weight = unpack(far)
        top = jnp.maximum(near_level, far_level)
        near_scale = jnp.exp2(near_level - top)
        far_scale = jnp.exp2(far_level - top)
        total = near_scale * near_weight + far_scale * far_weight
        near_scale = near_scale / total
        far_scale = far_scale / total
        for h in range(heads):
            place = slice(h * rows, (h + 1) * rows)
            mixed = near[0, place, :].astype(jnp.float32) * near_scale[:, h : h + 1]
            mixed = mixed + far[0, place, :].astype(jnp.float32) * far_scale[:, h : h + 1]
            mixtures.append((k, h, mixed.astype(out.dtype)))
    for k, h, mixed in mixtures:
        start = pl.multiple_of((member ^ k) * width + h * head, head)
        out[:, pl.ds(start, head)] = mixed


def merge(heads, near, far, rows):
    head = near[0].shape[2]
    return pl.pallas_call(
        functools.partial(merge_kernel, heads),
        out_shape=jax.ShapeDtypeStruct((rows, GROUP * heads * head), near[0].dtype),
        in_specs=[VMEM] * 8,
        out_specs=VMEM,
        compiler_params=limit(4 * MB),
        cost_estimate=cost(1000),
        name="merge",
    )(*near, *far)


def shards(queries, keys_new, values_new, keys_copy, values_copy, key_bounds, value_bounds):
    rows = queries.shape[0]
    heads = key_bounds.shape[1] // GROUP
    levels = lax.axis_size("patch").bit_length() - 1
    across = 1 << levels - 1

    pinned = [pltpu.with_memory_space_constraint(a, pltpu.HBM) for a in (keys_new, values_new, queries)]
    copies = [pltpu.with_memory_space_constraint(a, pltpu.HBM) for a in (keys_copy, values_copy)]
    sent = cut(1, pinned)
    beside = swapped(sent, 1)
    kept = cut(0, pinned, sent)
    x_query, x_keys, x_own, near_raw = join(kept, beside)
    own_query = assemble(kept, beside, swapped(x_query, 2))
    far_query = swapped(own_query, across)
    bits = [1 << bit for bit in range(2, levels - 1)]
    for bit in bits[:-1]:
        near_raw = jnp.concatenate([near_raw, swapped(near_raw, bit)], axis=1)
    far_raw = swapped(near_raw, bits[-1])
    if len(bits) > 1:
        x_own = near_raw[1]
    x_keys, x_own = swapped(x_keys, 2), swapped(x_own, 2)
    count = 1 << len(bits)
    old, limits = fetch(heads, rows, count, *copies, key_bounds, value_bounds)
    block = GROUP * rows
    rebuild_keys = functools.partial(rebuild_keys_kernel, heads)
    near_keys = rebuild(rebuild_keys, block, old, kept, beside, x_keys, old, limits, own_query)
    picked = pick(far_raw, near_keys)
    for bit in bits[:-1]:
        near_keys = jnp.concatenate([near_keys, swapped(near_keys, bit)], axis=0)
    far_keys = swapped(near_keys, bits[-1])
    halves = []
    sides = ((0, near_raw, x_own, own_query), (count // 2, far_raw, swapped(picked, 2), far_query))
    for first, this, opposite, earlier in sides:
        kernel = functools.partial(rebuild_values_kernel, heads, first)
        halves.append(rebuild(kernel, block * count // 2, old, this, opposite, old, limits, earlier))
    near, far = (near_keys, halves[0]), (far_keys, halves[1])
    parts = ((0,), (1,), (2, 3))
    n0, n1, n23 = attend(heads, parts, own_query, near, far)
    parts = ((2, 3), (0,), (1,))
    far_out = attend(heads, parts, far_query, near, far, n23)
    f23, f0, f1 = [swapped(a, across + group[0]) for a, group in zip(far_out, parts)]
    n1, n23 = swapped(n1, 1), swapped(n23, 2)
    f3 = pick(f23)
    n3 = pick(n23, f3)
    near_parts = (n0, n1, n23, swapped(n3, 1)[None])
    far_parts = (f0, f1, f23, swapped(f3, 1)[None])
    return merge(heads, near_parts, far_parts, rows)


def solution(mesh):
    rows = P(("clips", "patch"), None)
    copies = P(("clips", "patch"), None, None)
    bounds = P("clips", None)
    return jax.shard_map(
        shards,
        mesh=mesh,
        in_specs=(rows, rows, rows, copies, copies, bounds, bounds),
        out_specs=rows,
        check_vma=False,
    )
```

```python
import functools

import jax
import jax.numpy as jnp
from jax import lax
from jax.experimental import pallas as pl
from jax.experimental.pallas import tpu as pltpu
from jax.sharding import PartitionSpec as P

GROUP = 4
LOG2E = 1.4426950408889634
MB = 1 << 20
HBM = pl.BlockSpec(memory_space=pltpu.HBM)
VMEM = pl.BlockSpec(memory_space=pltpu.VMEM)


def limit(size):
    return pltpu.CompilerParams(vmem_limit_bytes=size)


def cost(size):
    return pl.CostEstimate(flops=0, bytes_accessed=size, transcendentals=0)


def swapped(array, mask):
    size = lax.axis_size("patch")
    return lax.ppermute(array, "patch", [(i, i ^ mask) for i in range(size)])


def position():
    place = lax.axis_index("patch")
    return place // GROUP, place % GROUP


def part(index, size):
    return pl.ds(pl.multiple_of(index * size, size), size)


def run_copies(pairs, sems):
    copies = [pltpu.make_async_copy(a, b, sems.at[i]) for i, (a, b) in enumerate(pairs)]
    for copy in copies:
        copy.start()
    for copy in copies:
        copy.wait()


def cut_kernel(count, first, *refs):
    slabs, out, sems = refs[:count], refs[-2], refs[-1]
    width = slabs[0].shape[1] // GROUP
    _, member = position()
    pairs = []
    for i, slab in enumerate(slabs):
        for k in range(2):
            pairs.append((slab.at[:, part(member ^ (first + 2 * k), width)], out.at[i, k]))
    run_copies(pairs, sems)


def cut(first, slabs, *earlier):
    rows, features = slabs[0].shape
    shape = jax.ShapeDtypeStruct((len(slabs), 2, rows, features // GROUP), slabs[0].dtype)
    return pl.pallas_call(
        functools.partial(cut_kernel, len(slabs), first),
        out_shape=shape,
        in_specs=[HBM] * (len(slabs) + len(earlier)),
        out_specs=VMEM,
        scratch_shapes=[pltpu.SemaphoreType.DMA((2 * len(slabs),))],
        compiler_params=limit(4 * MB),
        cost_estimate=cost(1000),
        name="cut",
    )(*slabs, *earlier)


def join_kernel(kept, arrived, x_query, x_keys, x_values, z_values):
    rows = kept.shape[2]
    for i, out in ((0, x_keys), (1, x_values), (2, x_query)):
        out[:rows] = kept[i, 1]
        out[rows:] = arrived[i, 1]
    for k in range(2):
        z_values[k, :rows] = kept[1, k]
        z_values[k, rows:] = arrived[1, k]


def join(kept, arrived):
    _, _, rows, width = kept.shape
    shape = (2 * rows, width)
    return pl.pallas_call(
        join_kernel,
        out_shape=[jax.ShapeDtypeStruct(shape, kept.dtype)] * 3 + [jax.ShapeDtypeStruct((2,) + shape, kept.dtype)],
        in_specs=[VMEM] * 2,
        out_specs=[VMEM] * 4,
        compiler_params=limit(4 * MB),
        cost_estimate=cost(1000),
        name="join",
    )(kept, arrived)


def assemble_kernel(kept, beside, opposite, out):
    rows = kept.shape[2]
    out[:rows] = kept[2, 0]
    out[rows : 2 * rows] = beside[2, 0]
    out[2 * rows :] = opposite[...]


def assemble(kept, beside, opposite):
    _, _, rows, width = kept.shape
    return pl.pallas_call(
        assemble_kernel,
        out_shape=jax.ShapeDtypeStruct((GROUP * rows, width), kept.dtype),
        in_specs=[VMEM] * 3,
        out_specs=VMEM,
        compiler_params=limit(4 * MB),
        cost_estimate=cost(1000),
        name="assemble",
    )(kept, beside, opposite)


def pick_kernel(both, *refs):
    refs[-1][...] = both[1]


def pick(both, *earlier):
    return pl.pallas_call(
        pick_kernel,
        out_shape=jax.ShapeDtypeStruct(both.shape[1:], both.dtype),
        in_specs=[VMEM] + [HBM] * len(earlier),
        out_specs=VMEM,
        compiler_params=limit(4 * MB + 2 * both.size * both.dtype.itemsize),
        cost_estimate=cost(4_000_000),
        name="pick",
    )(both, *earlier)


def fetch_kernel(heads, count, keys_copy, values_copy, kb, vb, old, limits, lines, turned, sems):
    rows = old.shape[1] // GROUP
    group, member = position()
    sources = [(keys_copy, kb, group)] + [(values_copy, vb, group ^ j) for j in range(count)]
    pairs = []
    for i, (copy, bound, block) in enumerate(sources):
        pairs.append((bound.at[:, part(block, GROUP * rows)], lines.at[i]))
        for k in range(GROUP):
            source = copy.at[0, part(block * GROUP + (member ^ k), rows), :]
            pairs.append((source, old.at[i, pl.ds(k * rows, rows), :]))
    run_copies(pairs, sems)
    for i in range(len(sources)):
        chosen = lines[i, pl.ds(member * heads, heads), :]
        padding = jnp.zeros((limits.shape[2] - heads, GROUP * rows), chosen.dtype)
        turned[...] = jnp.concatenate([chosen, padding], axis=0).T
        for k in range(GROUP):
            limits[i, pl.ds(k * rows, rows), :] = turned[part(member ^ k, rows), :]


def fetch(heads, rows, count, keys_copy, values_copy, key_bounds, value_bounds):
    width = keys_copy.shape[2]
    return pl.pallas_call(
        functools.partial(fetch_kernel, heads, count),
        out_shape=[
            jax.ShapeDtypeStruct((1 + count, GROUP * rows, width), keys_copy.dtype),
            jax.ShapeDtypeStruct((1 + count, GROUP * rows, 128), key_bounds.dtype),
        ],
        in_specs=[HBM] * 4,
        out_specs=[VMEM] * 2,
        scratch_shapes=[
            pltpu.VMEM((1 + count, key_bounds.shape[1], GROUP * rows), key_bounds.dtype),
            pltpu.VMEM((GROUP * rows, 128), key_bounds.dtype),
            pltpu.SemaphoreType.DMA(((1 + GROUP) * (1 + count),)),
        ],
        compiler_params=limit(4 * MB + MB * count),
        cost_estimate=cost(1000),
        name="fetch",
    )(keys_copy, values_copy, key_bounds.T, value_bounds.T)


def restore(heads, pieces, old, limits, out, start):
    rows, width = pieces[0].shape
    head = width // heads
    for k, piece in enumerate(pieces):
        place = slice(k * rows, (k + 1) * rows)
        for h in range(heads):
            lanes = slice(h * head, (h + 1) * head)
            bound = limits[place, h : h + 1]
            previous = old[place, lanes].astype(jnp.float32)
            change = jnp.clip(piece[:, lanes].astype(jnp.float32) - previous, -bound, bound)
            change = change.astype(jnp.bfloat16).astype(jnp.float32)
            out[start + k * rows : start + (k + 1) * rows, lanes] = (previous + change).astype(out.dtype)


def rebuild_keys_kernel(heads, kept, beside, opposite, old, limits, _, out):
    rows = kept.shape[2]
    pieces = [kept.at[0, 0], beside.at[0, 0], opposite.at[pl.ds(0, rows)], opposite.at[pl.ds(rows, rows)]]
    restore(heads, pieces, old.at[0], limits.at[0], out, 0)


def rebuild_values_kernel(heads, first, this, opposite, old, limits, *refs):
    out = refs[-1]
    rows = old.shape[1] // GROUP
    for j in range(this.shape[1] // (2 * rows)):
        starts = [2 * j * rows, (2 * j + 1) * rows]
        pieces = [this.at[0, pl.ds(start, rows)] for start in starts]
        pieces += [opposite.at[pl.ds(start, rows)] for start in starts]
        restore(heads, pieces, old.at[1 + first + j], limits.at[1 + first + j], out, j * GROUP * rows)


def rebuild(kernel, tokens, old, *operands):
    return pl.pallas_call(
        kernel,
        out_shape=jax.ShapeDtypeStruct((tokens, old.shape[2]), old.dtype),
        in_specs=[VMEM] * len(operands),
        out_specs=VMEM,
        compiler_params=limit(4 * MB + 16 * tokens * old.shape[2]),
        cost_estimate=cost(1000),
        name="rebuild",
    )(*operands)


def attend_kernel(heads, parts, query_ref, near_keys, near_values, far_keys, far_values, *refs):
    refs = refs[-len(parts) :]
    width = near_keys.shape[1]
    rows = query_ref.shape[0] // GROUP
    head = width // heads
    outs = {k: ref.at[j] for ref, group in zip(refs, parts) for j, k in enumerate(group)}
    scale = head ** (-0.5) * LOG2E
    lane = lax.broadcasted_iota(jnp.int32, (GROUP * rows, head), 1)
    stats = jnp.zeros((GROUP * rows, head), jnp.float32)
    contract = (((1,), (1,)), ((), ()))
    def stacked(near, far, h):
        lanes = slice(h * head, (h + 1) * head)
        return jnp.concatenate([near[:, lanes], far[:, lanes]], axis=0)

    scores = []
    for h in range(heads):
        query = query_ref[:, h * head : (h + 1) * head]
        keys = stacked(near_keys, far_keys, h)
        scores.append(lax.dot_general(query, keys, contract, preferred_element_type=jnp.float32))
    peaks = [jnp.max(score, axis=1, keepdims=True) for score in scores]
    levels = [(peak * scale).astype(jnp.bfloat16).astype(jnp.float32) for peak in peaks]
    probs = [jnp.exp2(score * scale - level).astype(jnp.bfloat16) for score, level in zip(scores, levels)]
    totals = []
    for h in range(heads):
        values = stacked(near_values, far_values, h)
        joined = jnp.concatenate([values, jnp.ones_like(values)], axis=1)
        totals.append(jnp.dot(probs[h], joined, preferred_element_type=jnp.float32))
    for h in range(heads):
        weight = totals[h][:, head:]
        high = weight.astype(jnp.bfloat16).astype(jnp.float32)
        stats = jnp.where(lane == h, levels[h], stats)
        stats = jnp.where(lane == heads + h, high, stats)
        stats = jnp.where(lane == 2 * heads + h, weight - high, stats)
    for h in range(heads):
        weighted = totals[h][:, :head].astype(jnp.bfloat16)
        for k, out in sorted(outs.items()):
            out[h * rows : (h + 1) * rows, :] = weighted[k * rows : (k + 1) * rows]
    half = rows // 2
    for k, out in sorted(outs.items()):
        first = stats[k * rows : k * rows + half]
        second = stats[k * rows + half : (k + 1) * rows]
        packed = first + pltpu.roll(second, 16, 1)
        out[heads * rows :, :] = packed.astype(out.dtype)


def attend(heads, parts, query, near, far, *earlier):
    tokens, width = near[0].shape
    rows = query.shape[0] // GROUP
    shape = (heads * rows + rows // 2, width // heads)
    outs = [jax.ShapeDtypeStruct((len(group),) + shape, near[0].dtype) for group in parts]
    room = 4 * MB + 32 * tokens * width + 64 * GROUP * rows * tokens
    return pl.pallas_call(
        functools.partial(attend_kernel, heads, parts),
        out_shape=outs,
        in_specs=[VMEM] * 5 + [HBM] * len(earlier),
        out_specs=[VMEM] * len(outs),
        compiler_params=limit(room),
        cost_estimate=cost(1000),
        name="attend",
    )(query, *near, *far, *earlier)


def merge_kernel(heads, n0, n1, n2, n3, f0, f1, f2, f3, out):
    rows = out.shape[0]
    head = n0.shape[2]
    width = heads * head
    _, member = position()

    def unpack(ref):
        packed = ref[0, heads * rows :, :].astype(jnp.float32)
        stats = jnp.concatenate([packed, pltpu.roll(packed, head - 16, 1)], axis=0)
        weight = pltpu.roll(stats, head - heads, 1) + pltpu.roll(stats, head - 2 * heads, 1)
        return stats, weight

    mixtures = []
    for k, (near, far) in enumerate(((n0, f0), (n1, f1), (n2, f2), (n3, f3))):
        near_level, near_weight = unpack(near)
        far_level, far_weight = unpack(far)
        top = jnp.maximum(near_level, far_level)
        near_scale = jnp.exp2(near_level - top)
        far_scale = jnp.exp2(far_level - top)
        total = near_scale * near_weight + far_scale * far_weight
        near_scale = near_scale / total
        far_scale = far_scale / total
        for h in range(heads):
            place = slice(h * rows, (h + 1) * rows)
            mixed = near[0, place, :].astype(jnp.float32) * near_scale[:, h : h + 1]
            mixed = mixed + far[0, place, :].astype(jnp.float32) * far_scale[:, h : h + 1]
            mixtures.append((k, h, mixed.astype(out.dtype)))
    for k, h, mixed in mixtures:
        start = pl.multiple_of((member ^ k) * width + h * head, head)
        out[:, pl.ds(start, head)] = mixed


def merge(heads, near, far, rows):
    head = near[0].shape[2]
    return pl.pallas_call(
        functools.partial(merge_kernel, heads),
        out_shape=jax.ShapeDtypeStruct((rows, GROUP * heads * head), near[0].dtype),
        in_specs=[VMEM] * 8,
        out_specs=VMEM,
        compiler_params=limit(4 * MB),
        cost_estimate=cost(1000),
        name="merge",
    )(*near, *far)


def shards(queries, keys_new, values_new, keys_copy, values_copy, key_bounds, value_bounds):
    rows = queries.shape[0]
    heads = key_bounds.shape[1] // GROUP
    levels = lax.axis_size("patch").bit_length() - 1
    across = 1 << levels - 1

    pinned = [pltpu.with_memory_space_constraint(a, pltpu.HBM) for a in (keys_new, values_new, queries)]
    copies = [pltpu.with_memory_space_constraint(a, pltpu.HBM) for a in (keys_copy, values_copy)]
    sent = cut(1, pinned)
    beside = swapped(sent, 1)
    kept = cut(0, pinned, sent)
    x_query, x_keys, x_own, near_raw = join(kept, beside)
    own_query = assemble(kept, beside, swapped(x_query, 2))
    far_query = swapped(own_query, across)
    bits = [1 << bit for bit in range(2, levels - 1)]
    for bit in bits[:-1]:
        near_raw = jnp.concatenate([near_raw, swapped(near_raw, bit)], axis=1)
    far_raw = swapped(near_raw, bits[-1])
    if len(bits) > 1:
        x_own = near_raw[1]
    x_keys, x_own = swapped(x_keys, 2), swapped(x_own, 2)
    count = 1 << len(bits)
    old, limits = fetch(heads, rows, count, *copies, key_bounds, value_bounds)
    block = GROUP * rows
    rebuild_keys = functools.partial(rebuild_keys_kernel, heads)
    near_keys = rebuild(rebuild_keys, block, old, kept, beside, x_keys, old, limits, own_query)
    picked = pick(far_raw, near_keys)
    for bit in bits[:-1]:
        near_keys = jnp.concatenate([near_keys, swapped(near_keys, bit)], axis=0)
    far_keys = swapped(near_keys, bits[-1])
    halves = []
    sides = ((0, near_raw, x_own, own_query), (count // 2, far_raw, swapped(picked, 2), far_query))
    for first, this, opposite, earlier in sides:
        kernel = functools.partial(rebuild_values_kernel, heads, first)
        halves.append(rebuild(kernel, block * count // 2, old, this, opposite, old, limits, earlier))
    near, far = (near_keys, halves[0]), (far_keys, halves[1])
    parts = ((2, 3), (0,), (1,))
    far_out = attend(heads, parts, far_query, near, far)
    f23, f0, f1 = [swapped(a, across + group[0]) for a, group in zip(far_out, parts)]
    parts = ((0,), (1,), (2, 3))
    n0, n1, n23 = attend(heads, parts, own_query, near, far, far_out[2])
    n1, n23 = swapped(n1, 1), swapped(n23, 2)
    f3 = pick(f23)
    n3 = pick(n23, f3)
    near_parts = (n0, n1, n23, swapped(n3, 1)[None])
    far_parts = (f0, f1, f23, swapped(f3, 1)[None])
    return merge(heads, near_parts, far_parts, rows)


def solution(mesh):
    rows = P(("clips", "patch"), None)
    copies = P(("clips", "patch"), None, None)
    bounds = P("clips", None)
    return jax.shard_map(
        shards,
        mesh=mesh,
        in_specs=(rows, rows, rows, copies, copies, bounds, bounds),
        out_specs=rows,
        check_vma=False,
    )
```

```python
import functools

import jax
import jax.numpy as jnp
from jax import lax
from jax.experimental import pallas as pl
from jax.experimental.pallas import tpu as pltpu
from jax.sharding import PartitionSpec as P

GROUP = 4
LOG2E = 1.4426950408889634
MB = 1 << 20
HBM = pl.BlockSpec(memory_space=pltpu.HBM)
VMEM = pl.BlockSpec(memory_space=pltpu.VMEM)


def limit(size):
    return pltpu.CompilerParams(vmem_limit_bytes=size)


def cost(size):
    return pl.CostEstimate(flops=0, bytes_accessed=size, transcendentals=0)


def swapped(array, mask):
    size = lax.axis_size("patch")
    return lax.ppermute(array, "patch", [(i, i ^ mask) for i in range(size)])


def position():
    place = lax.axis_index("patch")
    return place // GROUP, place % GROUP


def part(index, size):
    return pl.ds(pl.multiple_of(index * size, size), size)


def run_copies(pairs, sems):
    copies = [pltpu.make_async_copy(a, b, sems.at[i]) for i, (a, b) in enumerate(pairs)]
    for copy in copies:
        copy.start()
    for copy in copies:
        copy.wait()


def cut_kernel(count, first, *refs):
    slabs, out, sems = refs[:count], refs[-2], refs[-1]
    width = slabs[0].shape[1] // GROUP
    _, member = position()
    pairs = []
    for i, slab in enumerate(slabs):
        for k in range(2):
            pairs.append((slab.at[:, part(member ^ (first + 2 * k), width)], out.at[i, k]))
    run_copies(pairs, sems)


def cut(first, slabs, *earlier):
    rows, features = slabs[0].shape
    shape = jax.ShapeDtypeStruct((len(slabs), 2, rows, features // GROUP), slabs[0].dtype)
    return pl.pallas_call(
        functools.partial(cut_kernel, len(slabs), first),
        out_shape=shape,
        in_specs=[HBM] * (len(slabs) + len(earlier)),
        out_specs=VMEM,
        scratch_shapes=[pltpu.SemaphoreType.DMA((2 * len(slabs),))],
        compiler_params=limit(4 * MB),
        cost_estimate=cost(1000),
        name="cut",
    )(*slabs, *earlier)


def join_kernel(kept, arrived, x_query, x_keys, x_values, z_values):
    rows = kept.shape[2]
    for i, out in ((0, x_keys), (1, x_values), (2, x_query)):
        out[:rows] = kept[i, 1]
        out[rows:] = arrived[i, 1]
    for k in range(2):
        z_values[k, :rows] = kept[1, k]
        z_values[k, rows:] = arrived[1, k]


def join(kept, arrived):
    _, _, rows, width = kept.shape
    shape = (2 * rows, width)
    return pl.pallas_call(
        join_kernel,
        out_shape=[jax.ShapeDtypeStruct(shape, kept.dtype)] * 3 + [jax.ShapeDtypeStruct((2,) + shape, kept.dtype)],
        in_specs=[VMEM] * 2,
        out_specs=[VMEM] * 4,
        compiler_params=limit(4 * MB),
        cost_estimate=cost(1000),
        name="join",
    )(kept, arrived)


def assemble_kernel(kept, beside, opposite, out):
    rows = kept.shape[2]
    out[:rows] = kept[2, 0]
    out[rows : 2 * rows] = beside[2, 0]
    out[2 * rows :] = opposite[...]


def assemble(kept, beside, opposite):
    _, _, rows, width = kept.shape
    return pl.pallas_call(
        assemble_kernel,
        out_shape=jax.ShapeDtypeStruct((GROUP * rows, width), kept.dtype),
        in_specs=[VMEM] * 3,
        out_specs=VMEM,
        compiler_params=limit(4 * MB),
        cost_estimate=cost(1000),
        name="assemble",
    )(kept, beside, opposite)


def gate_kernel(array, _, out):
    out[...] = array[...]


def gate(array, earlier, size):
    return pl.pallas_call(
        gate_kernel,
        out_shape=jax.ShapeDtypeStruct(array.shape, array.dtype),
        in_specs=[VMEM, HBM],
        out_specs=VMEM,
        compiler_params=limit(4 * MB),
        cost_estimate=cost(size),
        name="gate",
    )(array, earlier)


def pick_kernel(both, *refs):
    refs[-1][...] = both[1]


def pick(both, *earlier):
    return pl.pallas_call(
        pick_kernel,
        out_shape=jax.ShapeDtypeStruct(both.shape[1:], both.dtype),
        in_specs=[VMEM] + [HBM] * len(earlier),
        out_specs=VMEM,
        compiler_params=limit(4 * MB + 2 * both.size * both.dtype.itemsize),
        cost_estimate=cost(4_000_000),
        name="pick",
    )(both, *earlier)


def fetch_kernel(heads, count, keys_copy, values_copy, kb, vb, old, limits, lines, turned, sems):
    rows = old.shape[1] // GROUP
    group, member = position()
    sources = [(keys_copy, kb, group)] + [(values_copy, vb, group ^ j) for j in range(count)]
    pairs = []
    for i, (copy, bound, block) in enumerate(sources):
        pairs.append((bound.at[:, part(block, GROUP * rows)], lines.at[i]))
        for k in range(GROUP):
            source = copy.at[0, part(block * GROUP + (member ^ k), rows), :]
            pairs.append((source, old.at[i, pl.ds(k * rows, rows), :]))
    run_copies(pairs, sems)
    for i in range(len(sources)):
        chosen = lines[i, pl.ds(member * heads, heads), :]
        padding = jnp.zeros((limits.shape[2] - heads, GROUP * rows), chosen.dtype)
        turned[...] = jnp.concatenate([chosen, padding], axis=0).T
        for k in range(GROUP):
            limits[i, pl.ds(k * rows, rows), :] = turned[part(member ^ k, rows), :]


def fetch(heads, rows, count, keys_copy, values_copy, key_bounds, value_bounds):
    width = keys_copy.shape[2]
    return pl.pallas_call(
        functools.partial(fetch_kernel, heads, count),
        out_shape=[
            jax.ShapeDtypeStruct((1 + count, GROUP * rows, width), keys_copy.dtype),
            jax.ShapeDtypeStruct((1 + count, GROUP * rows, 128), key_bounds.dtype),
        ],
        in_specs=[HBM] * 4,
        out_specs=[VMEM] * 2,
        scratch_shapes=[
            pltpu.VMEM((1 + count, key_bounds.shape[1], GROUP * rows), key_bounds.dtype),
            pltpu.VMEM((GROUP * rows, 128), key_bounds.dtype),
            pltpu.SemaphoreType.DMA(((1 + GROUP) * (1 + count),)),
        ],
        compiler_params=limit(4 * MB + MB * count),
        cost_estimate=cost(1000),
        name="fetch",
    )(keys_copy, values_copy, key_bounds.T, value_bounds.T)


def restore(heads, pieces, old, limits, out, start):
    rows, width = pieces[0].shape
    head = width // heads
    for k, piece in enumerate(pieces):
        place = slice(k * rows, (k + 1) * rows)
        for h in range(heads):
            lanes = slice(h * head, (h + 1) * head)
            bound = limits[place, h : h + 1]
            previous = old[place, lanes].astype(jnp.float32)
            change = jnp.clip(piece[:, lanes].astype(jnp.float32) - previous, -bound, bound)
            change = change.astype(jnp.bfloat16).astype(jnp.float32)
            out[start + k * rows : start + (k + 1) * rows, lanes] = (previous + change).astype(out.dtype)


def rebuild_keys_kernel(heads, kept, beside, opposite, old, limits, _, out):
    rows = kept.shape[2]
    pieces = [kept.at[0, 0], beside.at[0, 0], opposite.at[pl.ds(0, rows)], opposite.at[pl.ds(rows, rows)]]
    restore(heads, pieces, old.at[0], limits.at[0], out, 0)


def rebuild_values_kernel(heads, first, this, opposite, old, limits, *refs):
    out = refs[-1]
    rows = old.shape[1] // GROUP
    for j in range(this.shape[1] // (2 * rows)):
        starts = [2 * j * rows, (2 * j + 1) * rows]
        pieces = [this.at[0, pl.ds(start, rows)] for start in starts]
        pieces += [opposite.at[pl.ds(start, rows)] for start in starts]
        restore(heads, pieces, old.at[1 + first + j], limits.at[1 + first + j], out, j * GROUP * rows)


def rebuild(kernel, tokens, old, *operands):
    return pl.pallas_call(
        kernel,
        out_shape=jax.ShapeDtypeStruct((tokens, old.shape[2]), old.dtype),
        in_specs=[VMEM] * len(operands),
        out_specs=VMEM,
        compiler_params=limit(4 * MB + 16 * tokens * old.shape[2]),
        cost_estimate=cost(1000),
        name="rebuild",
    )(*operands)


def attend_kernel(heads, parts, query_ref, near_keys, near_values, far_keys, far_values, *refs):
    refs = refs[-len(parts) :]
    width = near_keys.shape[1]
    rows = query_ref.shape[0] // GROUP
    head = width // heads
    outs = {k: ref.at[j] for ref, group in zip(refs, parts) for j, k in enumerate(group)}
    scale = head ** (-0.5) * LOG2E
    lane = lax.broadcasted_iota(jnp.int32, (GROUP * rows, head), 1)
    stats = jnp.zeros((GROUP * rows, head), jnp.float32)
    contract = (((1,), (1,)), ((), ()))
    def stacked(near, far, h):
        lanes = slice(h * head, (h + 1) * head)
        return jnp.concatenate([near[:, lanes], far[:, lanes]], axis=0)

    scores = []
    for h in range(heads):
        query = query_ref[:, h * head : (h + 1) * head]
        keys = stacked(near_keys, far_keys, h)
        scores.append(lax.dot_general(query, keys, contract, preferred_element_type=jnp.float32))
    peaks = [jnp.max(score, axis=1, keepdims=True) for score in scores]
    levels = [(peak * scale).astype(jnp.bfloat16).astype(jnp.float32) for peak in peaks]
    probs = [jnp.exp2(score * scale - level).astype(jnp.bfloat16) for score, level in zip(scores, levels)]
    totals = []
    for h in range(heads):
        values = stacked(near_values, far_values, h)
        joined = jnp.concatenate([values, jnp.ones_like(values)], axis=1)
        totals.append(jnp.dot(probs[h], joined, preferred_element_type=jnp.float32))
    for h in range(heads):
        weight = totals[h][:, head:]
        high = weight.astype(jnp.bfloat16).astype(jnp.float32)
        stats = jnp.where(lane == h, levels[h], stats)
        stats = jnp.where(lane == heads + h, high, stats)
        stats = jnp.where(lane == 2 * heads + h, weight - high, stats)
    for h in range(heads):
        weighted = totals[h][:, :head].astype(jnp.bfloat16)
        for k, out in sorted(outs.items()):
            out[h * rows : (h + 1) * rows, :] = weighted[k * rows : (k + 1) * rows]
    half = rows // 2
    for k, out in sorted(outs.items()):
        first = stats[k * rows : k * rows + half]
        second = stats[k * rows + half : (k + 1) * rows]
        packed = first + pltpu.roll(second, 16, 1)
        out[heads * rows :, :] = packed.astype(out.dtype)


def attend(heads, parts, query, near, far, *earlier):
    tokens, width = near[0].shape
    rows = query.shape[0] // GROUP
    shape = (heads * rows + rows // 2, width // heads)
    outs = [jax.ShapeDtypeStruct((len(group),) + shape, near[0].dtype) for group in parts]
    room = 4 * MB + 32 * tokens * width + 64 * GROUP * rows * tokens
    return pl.pallas_call(
        functools.partial(attend_kernel, heads, parts),
        out_shape=outs,
        in_specs=[VMEM] * 5 + [HBM] * len(earlier),
        out_specs=[VMEM] * len(outs),
        compiler_params=limit(room),
        cost_estimate=cost(1000),
        name="attend",
    )(query, *near, *far, *earlier)


def merge_kernel(heads, n0, n1, n2, n3, f0, f1, f2, f3, out):
    rows = out.shape[0]
    head = n0.shape[2]
    width = heads * head
    _, member = position()

    def unpack(ref):
        packed = ref[0, heads * rows :, :].astype(jnp.float32)
        stats = jnp.concatenate([packed, pltpu.roll(packed, head - 16, 1)], axis=0)
        weight = pltpu.roll(stats, head - heads, 1) + pltpu.roll(stats, head - 2 * heads, 1)
        return stats, weight

    mixtures = []
    for k, (near, far) in enumerate(((n0, f0), (n1, f1), (n2, f2), (n3, f3))):
        near_level, near_weight = unpack(near)
        far_level, far_weight = unpack(far)
        top = jnp.maximum(near_level, far_level)
        near_scale = jnp.exp2(near_level - top)
        far_scale = jnp.exp2(far_level - top)
        total = near_scale * near_weight + far_scale * far_weight
        near_scale = near_scale / total
        far_scale = far_scale / total
        for h in range(heads):
            place = slice(h * rows, (h + 1) * rows)
            mixed = near[0, place, :].astype(jnp.float32) * near_scale[:, h : h + 1]
            mixed = mixed + far[0, place, :].astype(jnp.float32) * far_scale[:, h : h + 1]
            mixtures.append((k, h, mixed.astype(out.dtype)))
    for k, h, mixed in mixtures:
        start = pl.multiple_of((member ^ k) * width + h * head, head)
        out[:, pl.ds(start, head)] = mixed


def merge(heads, near, far, rows):
    head = near[0].shape[2]
    return pl.pallas_call(
        functools.partial(merge_kernel, heads),
        out_shape=jax.ShapeDtypeStruct((rows, GROUP * heads * head), near[0].dtype),
        in_specs=[VMEM] * 8,
        out_specs=VMEM,
        compiler_params=limit(4 * MB),
        cost_estimate=cost(1000),
        name="merge",
    )(*near, *far)


def shards(queries, keys_new, values_new, keys_copy, values_copy, key_bounds, value_bounds):
    rows = queries.shape[0]
    heads = key_bounds.shape[1] // GROUP
    levels = lax.axis_size("patch").bit_length() - 1
    across = 1 << levels - 1

    pinned = [pltpu.with_memory_space_constraint(a, pltpu.HBM) for a in (keys_new, values_new, queries)]
    copies = [pltpu.with_memory_space_constraint(a, pltpu.HBM) for a in (keys_copy, values_copy)]
    sent = cut(1, pinned)
    beside = swapped(sent, 1)
    kept = cut(0, pinned, sent)
    x_query, x_keys, x_own, near_raw = join(kept, beside)
    own_query = assemble(kept, beside, swapped(x_query, 2))
    far_query = swapped(own_query, across)
    bits = [1 << bit for bit in range(2, levels - 1)]
    for bit in bits[:-1]:
        near_raw = jnp.concatenate([near_raw, swapped(near_raw, bit)], axis=1)
    far_raw = swapped(near_raw, bits[-1])
    if len(bits) > 1:
        x_own = near_raw[1]
    x_keys, x_own = swapped(x_keys, 2), swapped(x_own, 2)
    count = 1 << len(bits)
    old, limits = fetch(heads, rows, count, *copies, key_bounds, value_bounds)
    block = GROUP * rows
    rebuild_keys = functools.partial(rebuild_keys_kernel, heads)
    near_keys = rebuild(rebuild_keys, block, old, kept, beside, x_keys, old, limits, own_query)
    picked = pick(far_raw, near_keys)
    for bit in bits[:-1]:
        near_keys = jnp.concatenate([near_keys, swapped(near_keys, bit)], axis=0)
    far_keys = swapped(near_keys, bits[-1])
    halves = []
    sides = ((0, near_raw, x_own, own_query), (count // 2, far_raw, swapped(picked, 2), own_query))
    for first, this, opposite, earlier in sides:
        kernel = functools.partial(rebuild_values_kernel, heads, first)
        halves.append(rebuild(kernel, block * count // 2, old, this, opposite, old, limits, earlier))
    far_query = gate(far_query, halves[1], 1000)
    near, far = (near_keys, halves[0]), (far_keys, halves[1])
    parts = ((2, 3), (0,), (1,))
    far_out = attend(heads, parts, far_query, near, far)
    f23, f0, f1 = [swapped(a, across + group[0]) for a, group in zip(far_out, parts)]
    parts = ((0,), (1,), (2, 3))
    n0, n1, n23 = attend(heads, parts, own_query, near, far, far_out[2])
    n1, n23 = swapped(n1, 1), swapped(n23, 2)
    f3 = pick(f23)
    n3 = pick(n23, f3)
    near_parts = (n0, n1, n23, swapped(n3, 1)[None])
    far_parts = (f0, f1, f23, swapped(f3, 1)[None])
    return merge(heads, near_parts, far_parts, rows)


def solution(mesh):
    rows = P(("clips", "patch"), None)
    copies = P(("clips", "patch"), None, None)
    bounds = P("clips", None)
    return jax.shard_map(
        shards,
        mesh=mesh,
        in_specs=(rows, rows, rows, copies, copies, bounds, bounds),
        out_specs=rows,
        check_vma=False,
    )
```

```python
import functools

import jax
import jax.numpy as jnp
from jax import lax
from jax.experimental import pallas as pl
from jax.experimental.pallas import tpu as pltpu
from jax.sharding import PartitionSpec as P

GROUP = 4
LOG2E = 1.4426950408889634
MB = 1 << 20
HBM = pl.BlockSpec(memory_space=pltpu.HBM)
VMEM = pl.BlockSpec(memory_space=pltpu.VMEM)


def limit(size):
    return pltpu.CompilerParams(vmem_limit_bytes=size)


def cost(size):
    return pl.CostEstimate(flops=0, bytes_accessed=size, transcendentals=0)


def swapped(array, mask):
    size = lax.axis_size("patch")
    return lax.ppermute(array, "patch", [(i, i ^ mask) for i in range(size)])


def position():
    place = lax.axis_index("patch")
    return place // GROUP, place % GROUP


def part(index, size):
    return pl.ds(pl.multiple_of(index * size, size), size)


def run_copies(pairs, sems):
    copies = [pltpu.make_async_copy(a, b, sems.at[i]) for i, (a, b) in enumerate(pairs)]
    for copy in copies:
        copy.start()
    for copy in copies:
        copy.wait()


def cut_kernel(count, *refs):
    slabs, sent, kept, sems = refs[:count], refs[-3], refs[-2], refs[-1]
    width = slabs[0].shape[1] // GROUP
    _, member = position()
    pairs = []
    for i, slab in enumerate(slabs):
        for k in range(2):
            pairs.append((slab.at[:, part(member ^ (1 + 2 * k), width)], sent.at[i, k]))
            pairs.append((slab.at[:, part(member ^ (2 * k), width)], kept.at[i, k]))
    run_copies(pairs, sems)


def cut(*slabs):
    rows, features = slabs[0].shape
    shape = jax.ShapeDtypeStruct((len(slabs), 2, rows, features // GROUP), slabs[0].dtype)
    return pl.pallas_call(
        functools.partial(cut_kernel, len(slabs)),
        out_shape=[shape] * 2,
        in_specs=[HBM] * len(slabs),
        out_specs=[VMEM] * 2,
        scratch_shapes=[pltpu.SemaphoreType.DMA((4 * len(slabs),))],
        compiler_params=limit(4 * MB),
        cost_estimate=cost(1000),
        name="cut",
    )(*slabs)


def join_kernel(kept, arrived, x_query, x_keys, x_values, z_values):
    rows = kept.shape[2]
    for i, out in ((0, x_keys), (1, x_values), (2, x_query)):
        out[:rows] = kept[i, 1]
        out[rows:] = arrived[i, 1]
    for k in range(2):
        z_values[k, :rows] = kept[1, k]
        z_values[k, rows:] = arrived[1, k]


def join(kept, arrived):
    _, _, rows, width = kept.shape
    shape = (2 * rows, width)
    return pl.pallas_call(
        join_kernel,
        out_shape=[jax.ShapeDtypeStruct(shape, kept.dtype)] * 3 + [jax.ShapeDtypeStruct((2,) + shape, kept.dtype)],
        in_specs=[VMEM] * 2,
        out_specs=[VMEM] * 4,
        compiler_params=limit(4 * MB),
        cost_estimate=cost(1000),
        name="join",
    )(kept, arrived)


def assemble_kernel(kept, beside, opposite, out):
    rows = kept.shape[2]
    out[:rows] = kept[2, 0]
    out[rows : 2 * rows] = beside[2, 0]
    out[2 * rows :] = opposite[...]


def assemble(kept, beside, opposite):
    _, _, rows, width = kept.shape
    return pl.pallas_call(
        assemble_kernel,
        out_shape=jax.ShapeDtypeStruct((GROUP * rows, width), kept.dtype),
        in_specs=[VMEM] * 3,
        out_specs=VMEM,
        compiler_params=limit(4 * MB),
        cost_estimate=cost(1000),
        name="assemble",
    )(kept, beside, opposite)


def gate_kernel(array, out):
    out[...] = array[...]


def gate(array):
    return pl.pallas_call(
        gate_kernel,
        out_shape=jax.ShapeDtypeStruct(array.shape, array.dtype),
        in_specs=[VMEM],
        out_specs=VMEM,
        compiler_params=limit(4 * MB),
        cost_estimate=cost(20_000_000),
        name="gate",
    )(array)


def pick_kernel(both, *refs):
    refs[-1][...] = both[1]


def pick(both, *earlier):
    return pl.pallas_call(
        pick_kernel,
        out_shape=jax.ShapeDtypeStruct(both.shape[1:], both.dtype),
        in_specs=[VMEM] + [HBM] * len(earlier),
        out_specs=VMEM,
        compiler_params=limit(4 * MB + 2 * both.size * both.dtype.itemsize),
        cost_estimate=cost(4_000_000),
        name="pick",
    )(both, *earlier)


def fetch_kernel(heads, count, keys_copy, values_copy, kb, vb, old, limits, lines, turned, sems):
    rows = old.shape[1] // GROUP
    group, member = position()
    sources = [(keys_copy, kb, group)] + [(values_copy, vb, group ^ j) for j in range(count)]
    pairs = []
    for i, (copy, bound, block) in enumerate(sources):
        pairs.append((bound.at[:, part(block, GROUP * rows)], lines.at[i]))
        for k in range(GROUP):
            source = copy.at[0, part(block * GROUP + (member ^ k), rows), :]
            pairs.append((source, old.at[i, pl.ds(k * rows, rows), :]))
    run_copies(pairs, sems)
    for i in range(len(sources)):
        chosen = lines[i, pl.ds(member * heads, heads), :]
        padding = jnp.zeros((limits.shape[2] - heads, GROUP * rows), chosen.dtype)
        turned[...] = jnp.concatenate([chosen, padding], axis=0).T
        for k in range(GROUP):
            limits[i, pl.ds(k * rows, rows), :] = turned[part(member ^ k, rows), :]


def fetch(heads, rows, count, keys_copy, values_copy, key_bounds, value_bounds):
    width = keys_copy.shape[2]
    return pl.pallas_call(
        functools.partial(fetch_kernel, heads, count),
        out_shape=[
            jax.ShapeDtypeStruct((1 + count, GROUP * rows, width), keys_copy.dtype),
            jax.ShapeDtypeStruct((1 + count, GROUP * rows, 128), key_bounds.dtype),
        ],
        in_specs=[HBM] * 4,
        out_specs=[VMEM] * 2,
        scratch_shapes=[
            pltpu.VMEM((1 + count, key_bounds.shape[1], GROUP * rows), key_bounds.dtype),
            pltpu.VMEM((GROUP * rows, 128), key_bounds.dtype),
            pltpu.SemaphoreType.DMA(((1 + GROUP) * (1 + count),)),
        ],
        compiler_params=limit(4 * MB + MB * count),
        cost_estimate=cost(1000),
        name="fetch",
    )(keys_copy, values_copy, key_bounds.T, value_bounds.T)


def restore(heads, pieces, old, limits, out, start):
    rows, width = pieces[0].shape
    head = width // heads
    for k, piece in enumerate(pieces):
        place = slice(k * rows, (k + 1) * rows)
        for h in range(heads):
            lanes = slice(h * head, (h + 1) * head)
            bound = limits[place, h : h + 1]
            previous = old[place, lanes].astype(jnp.float32)
            change = jnp.clip(piece[:, lanes].astype(jnp.float32) - previous, -bound, bound)
            change = change.astype(jnp.bfloat16).astype(jnp.float32)
            out[start + k * rows : start + (k + 1) * rows, lanes] = (previous + change).astype(out.dtype)


def rebuild_keys_kernel(heads, kept, beside, opposite, old, limits, _, out):
    rows = kept.shape[2]
    pieces = [kept.at[0, 0], beside.at[0, 0], opposite.at[pl.ds(0, rows)], opposite.at[pl.ds(rows, rows)]]
    restore(heads, pieces, old.at[0], limits.at[0], out, 0)


def rebuild_values_kernel(heads, first, this, opposite, old, limits, *refs):
    out = refs[-1]
    rows = old.shape[1] // GROUP
    for j in range(this.shape[1] // (2 * rows)):
        starts = [2 * j * rows, (2 * j + 1) * rows]
        pieces = [this.at[0, pl.ds(start, rows)] for start in starts]
        pieces += [opposite.at[pl.ds(start, rows)] for start in starts]
        restore(heads, pieces, old.at[1 + first + j], limits.at[1 + first + j], out, j * GROUP * rows)


def rebuild(kernel, tokens, old, *operands):
    return pl.pallas_call(
        kernel,
        out_shape=jax.ShapeDtypeStruct((tokens, old.shape[2]), old.dtype),
        in_specs=[VMEM] * len(operands),
        out_specs=VMEM,
        compiler_params=limit(4 * MB + 16 * tokens * old.shape[2]),
        cost_estimate=cost(1000),
        name="rebuild",
    )(*operands)


def attend_kernel(heads, parts, query_ref, near_keys, near_values, far_keys, far_values, *refs):
    refs = refs[-len(parts) :]
    width = near_keys.shape[1]
    rows = query_ref.shape[0] // GROUP
    head = width // heads
    outs = {k: ref.at[j] for ref, group in zip(refs, parts) for j, k in enumerate(group)}
    scale = head ** (-0.5) * LOG2E
    lane = lax.broadcasted_iota(jnp.int32, (GROUP * rows, head), 1)
    stats = jnp.zeros((GROUP * rows, head), jnp.float32)
    contract = (((1,), (1,)), ((), ()))
    def stacked(near, far, h):
        lanes = slice(h * head, (h + 1) * head)
        return jnp.concatenate([near[:, lanes], far[:, lanes]], axis=0)

    scores = []
    for h in range(heads):
        query = query_ref[:, h * head : (h + 1) * head]
        keys = stacked(near_keys, far_keys, h)
        scores.append(lax.dot_general(query, keys, contract, preferred_element_type=jnp.float32))
    peaks = [jnp.max(score, axis=1, keepdims=True) for score in scores]
    levels = [(peak * scale).astype(jnp.bfloat16).astype(jnp.float32) for peak in peaks]
    probs = [jnp.exp2(score * scale - level).astype(jnp.bfloat16) for score, level in zip(scores, levels)]
    totals = []
    for h in range(heads):
        values = stacked(near_values, far_values, h)
        joined = jnp.concatenate([values, jnp.ones_like(values)], axis=1)
        totals.append(jnp.dot(probs[h], joined, preferred_element_type=jnp.float32))
    for h in range(heads):
        weight = totals[h][:, head:]
        high = weight.astype(jnp.bfloat16).astype(jnp.float32)
        stats = jnp.where(lane == h, levels[h], stats)
        stats = jnp.where(lane == heads + h, high, stats)
        stats = jnp.where(lane == 2 * heads + h, weight - high, stats)
    for h in range(heads):
        weighted = totals[h][:, :head].astype(jnp.bfloat16)
        for k, out in sorted(outs.items()):
            out[h * rows : (h + 1) * rows, :] = weighted[k * rows : (k + 1) * rows]
    half = rows // 2
    for k, out in sorted(outs.items()):
        first = stats[k * rows : k * rows + half]
        second = stats[k * rows + half : (k + 1) * rows]
        packed = first + pltpu.roll(second, 16, 1)
        out[heads * rows :, :] = packed.astype(out.dtype)


def attend(heads, parts, query, near, far, *earlier):
    tokens, width = near[0].shape
    rows = query.shape[0] // GROUP
    shape = (heads * rows + rows // 2, width // heads)
    outs = [jax.ShapeDtypeStruct((len(group),) + shape, near[0].dtype) for group in parts]
    room = 4 * MB + 32 * tokens * width + 64 * GROUP * rows * tokens
    return pl.pallas_call(
        functools.partial(attend_kernel, heads, parts),
        out_shape=outs,
        in_specs=[VMEM] * 5 + [HBM] * len(earlier),
        out_specs=[VMEM] * len(outs),
        compiler_params=limit(room),
        cost_estimate=cost(1000),
        name="attend",
    )(query, *near, *far, *earlier)


def unpack(ref, heads, rows):
    head = ref.shape[2]
    packed = ref[0, heads * rows :, :].astype(jnp.float32)
    stats = jnp.concatenate([packed, pltpu.roll(packed, head - 16, 1)], axis=0)
    weight = pltpu.roll(stats, head - heads, 1) + pltpu.roll(stats, head - 2 * heads, 1)
    return stats, weight


def mix(heads, near, far, out):
    rows, width = out.shape
    head = width // heads
    near_level, near_weight = unpack(near, heads, rows)
    far_level, far_weight = unpack(far, heads, rows)
    top = jnp.maximum(near_level, far_level)
    near_scale = jnp.exp2(near_level - top)
    far_scale = jnp.exp2(far_level - top)
    total = near_scale * near_weight + far_scale * far_weight
    near_scale = near_scale / total
    far_scale = far_scale / total
    for h in range(heads):
        place = slice(h * rows, (h + 1) * rows)
        mixed = near[0, place, :].astype(jnp.float32) * near_scale[:, h : h + 1]
        mixed = mixed + far[0, place, :].astype(jnp.float32) * far_scale[:, h : h + 1]
        out[:, h * head : (h + 1) * head] = mixed.astype(out.dtype)


def mix_kernel(heads, n2, f2, n3, f3, out):
    mix(heads, n2, f2, out.at[0])
    mix(heads, n3, f3, out.at[1])


def merge_kernel(heads, n0, f0, n1, f1, done, out, mixture, sems):
    _, member = position()
    width = mixture.shape[2]
    copies = []
    for k in (2, 3, 0, 1):
        if k < 2:
            mix(heads, (n0, n1)[k], (f0, f1)[k], mixture.at[k])
        source = mixture.at[k] if k < 2 else done.at[k - 2]
        copies.append(pltpu.make_async_copy(source, out.at[:, part(member ^ k, width)], sems.at[k]))
        copies[-1].start()
    for copy in copies:
        copy.wait()


def merge(heads, near, far, rows):
    head = near[0].shape[2]
    kind = near[0].dtype
    half = (2, rows, heads * head)
    done = pl.pallas_call(
        functools.partial(mix_kernel, heads),
        out_shape=jax.ShapeDtypeStruct(half, kind),
        in_specs=[VMEM] * 4,
        out_specs=VMEM,
        compiler_params=limit(4 * MB),
        cost_estimate=cost(1000),
        name="mix",
    )(near[2], far[2], near[3], far[3])
    return pl.pallas_call(
        functools.partial(merge_kernel, heads),
        out_shape=jax.ShapeDtypeStruct((rows, GROUP * heads * head), kind),
        in_specs=[VMEM] * 5,
        out_specs=HBM,
        scratch_shapes=[pltpu.VMEM(half, kind), pltpu.SemaphoreType.DMA((GROUP,))],
        compiler_params=limit(4 * MB),
        cost_estimate=cost(1000),
        name="merge",
    )(near[0], far[0], near[1], far[1], done)


def shards(queries, keys_new, values_new, keys_copy, values_copy, key_bounds, value_bounds):
    rows = queries.shape[0]
    heads = key_bounds.shape[1] // GROUP
    levels = lax.axis_size("patch").bit_length() - 1
    across = 1 << levels - 1

    pinned = [pltpu.with_memory_space_constraint(a, pltpu.HBM) for a in (keys_new, values_new, queries)]
    copies = [pltpu.with_memory_space_constraint(a, pltpu.HBM) for a in (keys_copy, values_copy)]
    sent, kept = cut(*pinned)
    beside = swapped(sent, 1)
    x_query, x_keys, x_own, near_raw = join(kept, beside)
    own_query = assemble(kept, beside, swapped(x_query, 2))
    far_query = swapped(own_query, across)
    bits = [1 << bit for bit in range(2, levels - 1)]
    for bit in bits[:-1]:
        near_raw = jnp.concatenate([near_raw, swapped(near_raw, bit)], axis=1)
    far_raw = swapped(near_raw, bits[-1])
    if len(bits) > 1:
        x_own = near_raw[1]
    x_keys, x_own = swapped(x_keys, 2), swapped(x_own, 2)
    count = 1 << len(bits)
    old, limits = fetch(heads, rows, count, *copies, key_bounds, value_bounds)
    block = GROUP * rows
    rebuild_keys = functools.partial(rebuild_keys_kernel, heads)
    near_keys = rebuild(rebuild_keys, block, old, kept, beside, x_keys, old, limits, own_query)
    picked = pick(far_raw, near_keys)
    for bit in bits[:-1]:
        near_keys = jnp.concatenate([near_keys, swapped(near_keys, bit)], axis=0)
    far_keys = swapped(near_keys, bits[-1])
    halves = []
    sides = ((0, near_raw, x_own, own_query), (count // 2, far_raw, swapped(picked, 2), far_query))
    for first, this, opposite, earlier in sides:
        kernel = functools.partial(rebuild_values_kernel, heads, first)
        halves.append(rebuild(kernel, block * count // 2, old, this, opposite, old, limits, earlier))
    near, far = (near_keys, halves[0]), (far_keys, halves[1])
    parts = ((2, 3), (0,), (1,))
    far_out = attend(heads, parts, far_query, near, far)
    f23, f0, f1 = [swapped(a, across + group[0]) for a, group in zip(far_out, parts)]
    parts = ((0,), (1,), (2, 3))
    n0, n1, n23 = attend(heads, parts, own_query, near, far, far_out[2])
    n1, n23 = swapped(n1, 1), swapped(n23, 2)
    f3 = pick(f23)
    n3 = pick(n23, f3)
    near_parts = (n0, gate(n1), n23, swapped(n3, 1)[None])
    far_parts = (gate(f0), gate(f1), f23, swapped(f3, 1)[None])
    return merge(heads, near_parts, far_parts, rows)


def solution(mesh):
    rows = P(("clips", "patch"), None)
    copies = P(("clips", "patch"), None, None)
    bounds = P("clips", None)
    return jax.shard_map(
        shards,
        mesh=mesh,
        in_specs=(rows, rows, rows, copies, copies, bounds, bounds),
        out_specs=rows,
        check_vma=False,
    )
```
